768 devices in a mesh: band: 32 (over y, z_lo), dom: 24 (over z_hi, x, core).
Axes of the slice: x: 4, y: 8, z: 12 (z_hi: 3, z_lo: 4; z = z_hi * 4 + z_lo), core: 2. Of those that a mesh axis runs over, the one named last changes fastest.
Arguments:
- states_in: float32 [256, 73728], P('band', 'dom'), may hold values from -6 to 6
- cell_nodes: int32 [384, 343], P('dom'), may hold values from 0 to 3839, as said below
- cell_scale: float32 [384], P('dom'), may hold values from 0.3 to 3
- cell_matrix: bfloat16 [343, 343], replicated
- node_scale: float32 [73728], P('dom'), may hold values from 0.5 to 2
- potential: float32 [73728], P('dom'), may hold values from -1 to 1
Outputs:
- filtered: bfloat16 [256, 73728], P('band', 'dom')
- gram: float32 [256, 256], P('band')
The draws below stay inside these ranges and needn't reach their ends.
Inputs may be any that keep to these rules, and one draw needn't show every extreme that they name: `cell_nodes`: each cell's nodes lie within its own domain's owned nodes and the 384-node rims of the two neighbouring domains; the first cell of every domain touches its lower rim's first node and the last cell its upper rim's last node.
All inputs are finite; a program needn't handle non-finite values.
Results may differ from the reference program's by a relative error of at most 0.0075.
Values may be sent and summed in bfloat16 or wider, within the bound.
A program may use at most 32 MiB of HBM per device.

```python
import math
import jax
import jax.numpy as jnp
from jax import lax

STATES = 256
NPC = 343
DEGREE = 3
NODE_DEV = 3072
GHOST = 384
CELL_DEV = 16
NODES = 73728
CELLS = 384
N_BAND = 32


def draw_cell_nodes(key, part):
    key = jax.random.fold_in(key, 11)
    span_len = 2 * GHOST
    extended_len = NODE_DEV + 2 * GHOST
    position = jnp.arange(CELLS, dtype=jnp.int32) % CELL_DEV
    base_node = position * (extended_len - span_len) // (CELL_DEV - 1)
    offsets = jax.random.randint(key, (CELLS, NPC), 0, span_len, dtype=jnp.int32)
    column = jnp.arange(NPC, dtype=jnp.int32)[None, :]
    offsets = jnp.where(column == 0, 0, offsets)
    offsets = jnp.where(column == NPC - 1, span_len - 1, offsets)
    return (base_node[:, None] + offsets).astype(jnp.int32)


def draw_cell_matrix(key, part):
    key = jax.random.fold_in(key, 23)
    raw = jax.random.normal(key, (NPC, NPC), jnp.float32)
    symmetric = (raw + raw.T) * (0.7 / NPC ** 0.5)
    return symmetric.astype(jnp.bfloat16)


def block_levels(stream_key, shape, pieces, least, top_value):
    factor_of = 1.0
    for axis_at, shards_of in pieces:
        steps = jax.random.uniform(jax.random.fold_in(jax.random.fold_in(stream_key, 6), axis_at), (shards_of,), jnp.float32, least / len(pieces), top_value / len(pieces))
        factor_of = factor_of * jnp.repeat(jnp.exp(steps), shape[axis_at] // shards_of).reshape((-1,) + (1,) * (len(shape) - 1 - axis_at))
    return factor_of


def bell_draw(own_key, extent, spread, reach, shards=(), kind=jnp.bfloat16):
    gain = block_levels(own_key, extent, shards, -0.22, 0.18) if shards else 1.0
    drawn = jax.random.normal(own_key, extent, jnp.float32) * spread * gain
    return jnp.minimum(jnp.maximum(drawn, -reach), reach).astype(kind)


def setup_inputs(seed: int = 0) -> dict:
    seeds = jax.random.split(jax.random.key(seed), 7)
    return {
        "states_in": bell_draw(seeds[0], (STATES, NODES), 1.0, 6.0, ((0, 32), (1, 24)), jnp.float32),
        "cell_nodes": draw_cell_nodes(jax.random.fold_in(seeds[6], 71), 0),
        "cell_scale": jnp.clip(jnp.exp(math.log(3.0) - 2.3025851 * jax.random.uniform(seeds[2], (CELLS,), jnp.float32) ** block_levels(seeds[2], (CELLS,), ((0, 24),), -0.2, 0.2)), 0.3, 3.0),
        "cell_matrix": draw_cell_matrix(jax.random.fold_in(seeds[6], 71), 0),
        "node_scale": jnp.clip(jnp.exp(math.log(2.0) - 1.3862944 * jax.random.uniform(seeds[4], (NODES,), jnp.float32) ** block_levels(seeds[4], (NODES,), ((0, 24),), -0.2, 0.2)), 0.5, 2.0),
        "potential": jnp.clip(jax.random.uniform(seeds[5], (NODES,), jnp.float32, -1.0, 1.0) * block_levels(seeds[5], (NODES,), ((0, 24),), -0.4, 0.0), -1.0, 1.0),
    }


filter_center = 0.25
filter_half = 1.5


def apply_hamiltonian(vector_in, global_nodes, cell_scale, cell_matrix, node_scale, potential):
    weighted = (node_scale[None, :] * vector_in).astype(jnp.bfloat16)
    padded = jnp.pad(weighted, ((0, 0), (GHOST, GHOST)))
    picked = padded[:, global_nodes]
    cellwise = jnp.einsum("ij,scj->sci", cell_matrix.astype(jnp.float32), picked.astype(jnp.float32))
    cellwise = cellwise * cell_scale[None, :, None]
    assembled = jnp.zeros(padded.shape, jnp.float32).at[:, global_nodes].add(cellwise)
    owned = assembled[:, GHOST:GHOST + NODES]
    return node_scale[None, :] * owned + potential[None, :] * vector_in


def reference(states_in, cell_nodes, cell_scale, cell_matrix, node_scale, potential):
    domain_of = (jnp.arange(CELLS, dtype=jnp.int32) // CELL_DEV).astype(jnp.int32)
    global_nodes = (cell_nodes + (domain_of * NODE_DEV)[:, None]).astype(jnp.int32)
    group_size = STATES // N_BAND

    def apply_one(vector_in):
        return apply_hamiltonian(vector_in, global_nodes, cell_scale, cell_matrix, node_scale, potential)

    def filter_group(group):
        previous = group
        current = (apply_one(group) - filter_center * group) / filter_half
        for step in range(DEGREE - 1):
            following = 2.0 * (apply_one(current) - filter_center * current) / filter_half - previous
            previous = current
            current = following
        return current.astype(jnp.bfloat16)

    groups = states_in.reshape(N_BAND, group_size, NODES)
    filtered = lax.map(filter_group, groups).reshape(STATES, NODES)
    gram = jnp.dot(filtered, filtered.T, preferred_element_type=jnp.float32) / NODES
    return filtered, gram
```

```python
import functools

import jax
import jax.numpy as jnp
from jax import lax
from jax.experimental import pallas as pl
from jax.experimental.pallas import tpu as pltpu
from jax.sharding import PartitionSpec as P

CENTER = 0.25
HALF = 1.5
MESH = pl.DeviceIdType.MESH
F32 = jnp.float32
BF16 = jnp.bfloat16

RIM_HI = (0, 1, 2, 3, 12, 13, 14, 15)
MID_HI = (4, 5, 6, 7, 8, 9, 10, 11)
LOW_TILES = ((0, 1), (1, 0), (1, 1), (2, 0), (2, 1), (3, 0))
UP_TILES = ((12, 1), (13, 0), (13, 1), (14, 0), (14, 1), (15, 0))
OWN_TILES = tuple((2 + t // 2, t % 2) for t in range(24))


def tile(ref, hi, half):
    return ref[8 * hi : 8 * hi + 8, 128 * half : 128 * half + 128]


def put(ref, hi, half, value):
    ref[8 * hi : 8 * hi + 8, 128 * half : 128 * half + 128] = value


def dot_t(a, b):
    return lax.dot_general(a, b, (((1,), (1,)), ((), ())), preferred_element_type=F32)


class Layout:
    def __init__(self, n_band, n_dom):
        self.n_band, self.n_dom = n_band, n_dom
        self.nz = 4 if n_band == 32 else 2
        self.ny = n_band // self.nz
        self.nx = 8 if n_dom == 24 else 2
        self.nh = n_dom // self.nx
        self.per = 24 // self.ny


def kernel(
    lay, nodes_all,
    states, nodes, cell_scale, matrix, node_scale, potential,
    filtered, gram,
    lt, le, mat, pad_nodes, hb, y0, y1, y2, ns, pc, acc, w2, mid, picked, x16, vh,
    stage, init_in, out_low, out_up, in_low, in_up, shares, got, part, part_in, sum1, sum1_in, sum2, sum2_in,
    send_sem, recv_sem, gram_send, gram_recv,
):
    band, dom = lax.axis_index("band"), lax.axis_index("dom")
    n_band, n_dom = lay.n_band, lay.n_dom
    left, right = lax.rem(dom + n_dom - 1, n_dom), lax.rem(dom + 1, n_dom)
    my_y, my_z = band // lay.nz, lax.rem(band, lay.nz)
    my_h, my_x = dom // lay.nx, lax.rem(dom, lay.nx)
    has_left, has_right = dom > 0, dom < n_dom - 1

    band_peers = [lax.rem(band + i, n_band) for i in range(1, n_band)]
    x_peers = [my_h * lay.nx + lax.rem(my_x + i, lay.nx) for i in range(1, lay.nx)]
    h_peers = [lax.rem(my_h + i, lay.nh) * lay.nx + my_x for i in range(1, lay.nh)]

    barrier = pltpu.get_barrier_semaphore()
    dom_peers = [left, right] + x_peers + h_peers
    for peer in dom_peers:
        pl.semaphore_signal(barrier, inc=1, device_id=(band, peer), device_id_type=MESH)
    for peer in band_peers:
        pl.semaphore_signal(barrier, inc=1, device_id=(peer, dom), device_id_type=MESH)

    pad_nodes[...] = jnp.full(pad_nodes.shape, -4096, jnp.int32)
    pad_nodes[:16, :343] = nodes[...]
    mat[...] = jnp.zeros(mat.shape, BF16)
    mat[:343, :343] = matrix[...]
    shifted = pad_nodes[...] + 128
    lo_all = shifted & 255
    hi_all = shifted >> 8
    lo_t = lo_all.T
    row_iota = lax.broadcasted_iota(jnp.int32, (256, 768), 0)
    lane_iota = lax.broadcasted_iota(jnp.int32, (384, 256), 1)
    for p in range(8):
        cols = slice(768 * p, 768 * p + 768)
        lo = jnp.concatenate([lo_all[2 * p : 2 * p + 1], lo_all[2 * p + 1 : 2 * p + 2]], axis=1)
        hi = jnp.concatenate([hi_all[2 * p : 2 * p + 1], hi_all[2 * p + 1 : 2 * p + 2]], axis=1)
        hb[p] = jnp.broadcast_to(hi, (8, 768))
        lt[:, cols] = jnp.where(row_iota == lo, 1.0, 0.0).astype(BF16)
        for c in (2 * p, 2 * p + 1):
            le[384 * c : 384 * c + 384, :] = jnp.where(
                lane_iota == lo_t[:, c : c + 1], 1.0, 0.0
            ).astype(BF16)

    for ref in (y0, ns, pc):
        ref[0:16] = jnp.zeros((16, 256), F32)
        ref[112:128] = jnp.zeros((16, 256), F32)
    for b in range(12):
        rows, cols = slice(16 + 8 * b, 24 + 8 * b), slice(256 * b, 256 * b + 256)
        y0[rows] = states[:, cols]
        ns[rows] = jnp.broadcast_to(node_scale[:, cols], (8, 256))
        pc[rows] = jnp.broadcast_to(potential[:, cols] - CENTER, (8, 256))
    for side, cols in ((0, slice(0, 384)), (1, slice(2688, 3072))):
        stage[side, 0:8] = states[:, cols]
        stage[side, 8:16] = jnp.concatenate(
            [node_scale[:, cols], potential[:, cols], jnp.zeros((6, 384), F32)], axis=0
        )

    pl.semaphore_wait(barrier, len(dom_peers) + len(band_peers))

    def rim_copy(src, dst, slot, to):
        copy = pltpu.make_async_remote_copy(
            src_ref=src, dst_ref=dst, send_sem=send_sem.at[slot], recv_sem=recv_sem.at[slot],
            device_id=(band, to), device_id_type=MESH,
        )
        copy.start()
        return copy

    started = [
        rim_copy(stage.at[0], init_in.at[1], 0, left),
        rim_copy(stage.at[1], init_in.at[0], 1, right),
    ]

    def gather(his, first):
        runs = [(his[0], his[-1] + 1)] if his == MID_HI else [(0, 4), (12, 16)]
        left_side = jnp.concatenate([w2[8 * a : 8 * b, :] for a, b in runs], axis=0)
        for p in range(8):
            cols = slice(768 * p, 768 * p + 768)
            t = jnp.dot(left_side, lt[:, cols], preferred_element_type=F32)
            index = hb[p]
            total = jnp.zeros((8, 768), F32) if first else mid[:, cols]
            for k, hi in enumerate(his):
                total = jnp.where(index == hi, t[8 * k : 8 * k + 8], total)
            if first:
                mid[:, cols] = total
            else:
                picked[16 * p : 16 * p + 16, :] = jnp.concatenate(
                    [total[:, :384], total[:, 384:]], axis=0
                ).astype(BF16)

    def scatter(his):
        for p in range(8):
            cols = slice(768 * p, 768 * p + 768)
            index = jnp.concatenate([hb[p], hb[p]], axis=0)
            x = x16[:, cols]
            for k, hi in enumerate(his):
                vh[16 * k : 16 * k + 16, cols] = jnp.where(index == hi, x, 0.0).astype(BF16)
        r = jnp.dot(vh[...], le[...], preferred_element_type=F32)
        for k, hi in enumerate(his):
            acc[8 * hi : 8 * hi + 8, :] = r[16 * k : 16 * k + 8] + r[16 * k + 8 : 16 * k + 16]

    def weigh(y, rows):
        w2[rows, :] = (ns[rows, :] * y[rows, :]).astype(BF16)

    def advance(step, rows, cols):
        now = (y0, y1, y2)[step][rows, cols]
        h = ns[rows, cols] * acc[rows, cols] + pc[rows, cols] * now
        if step == 0:
            y1[rows, cols] = h * (1.0 / HALF)
        elif step == 1:
            y2[rows, cols] = h * (2.0 / HALF) - y0[rows, cols]
        else:
            y1[rows, cols] = h * (2.0 / HALF) - y1[rows, cols]

    whole = slice(0, 256)
    middle, lower, upper = slice(32, 96), slice(0, 32), slice(96, 128)

    weigh(y0, middle)
    gather(MID_HI, True)
    for copy in started:
        copy.wait_recv()
    for side, tiles in ((0, LOW_TILES[:3]), (1, UP_TILES[3:])):
        there = has_left if side == 0 else has_right
        value = jnp.where(there, init_in[side], 0.0)
        for i, (hi, half) in enumerate(tiles):
            cols = slice(128 * i, 128 * i + 128)
            put(y0, hi, half, value[0:8, cols])
            put(ns, hi, half, jnp.broadcast_to(value[8:9, cols], (8, 128)))
            put(pc, hi, half, jnp.broadcast_to(value[9:10, cols] - CENTER, (8, 128)))
    weigh(y0, lower)
    weigh(y0, upper)
    gather(RIM_HI, False)

    gram_copies = []

    def send_share(share):
        for z in range(lay.nz):
            def go(share=share, z=z):
                pltpu.make_async_remote_copy(
                    src_ref=shares.at[share], dst_ref=got.at[band],
                    send_sem=gram_send.at[0], recv_sem=gram_recv.at[0],
                    device_id=(share * lay.nz + z, dom), device_id_type=MESH,
                ).start()
            pl.when(band != share * lay.nz + z)(go)

    def fill_shares(which):
        for share in which:
            tiles = OWN_TILES[lay.per * share : lay.per * share + lay.per]
            shares[share] = jnp.concatenate([tile(y1, *t) for t in tiles], axis=1).astype(BF16)
            filtered[:, 128 * lay.per * share : 128 * lay.per * (share + 1)] = shares[share]
            send_share(share)

    for step in range(3):
        cells = dot_t(picked[...], mat[...])
        for p in range(8):
            x = jnp.concatenate(
                [cells[16 * p : 16 * p + 8] * cell_scale[2 * p],
                 cells[16 * p + 8 : 16 * p + 16] * cell_scale[2 * p + 1]], axis=1)
            rest = x - x.astype(BF16).astype(F32)
            x16[:, 768 * p : 768 * p + 768] = jnp.concatenate([x, rest], axis=0)
        scatter(RIM_HI)
        last = step == 2
        low_tiles, up_tiles = (LOW_TILES[:3], UP_TILES[3:]) if last else (LOW_TILES, UP_TILES)
        for i, (lt_, ut_) in enumerate(zip(low_tiles, up_tiles)):
            out_low[step, 8 * i : 8 * i + 8] = tile(acc, *lt_)
            out_up[step, 8 * i : 8 * i + 8] = tile(acc, *ut_)
        rows = 8 * len(low_tiles)
        now = [
            rim_copy(out_low.at[step, 0:rows], in_up.at[step, 0:rows], 2 + 2 * step, left),
            rim_copy(out_up.at[step, 0:rows], in_low.at[step, 0:rows], 3 + 2 * step, right),
        ]
        started += now
        scatter(MID_HI)
        advance(step, middle, whole)
        if last:
            advance(step, slice(24, 32), slice(128, 256))
            advance(step, slice(96, 104), slice(0, 128))
            fill_shares(range(1, lay.ny - 1))
        else:
            weigh((y1, y2)[step], middle)
            gather(MID_HI, True)
        for copy in now:
            copy.wait_recv()
        low_to, up_to = (LOW_TILES[3:], UP_TILES[:3]) if last else (LOW_TILES, UP_TILES)
        for i, (lt_, ut_) in enumerate(zip(low_to, up_to)):
            got_low = jnp.where(has_left, in_low[step, 8 * i : 8 * i + 8], 0.0)
            got_up = jnp.where(has_right, in_up[step, 8 * i : 8 * i + 8], 0.0)
            put(acc, *lt_, tile(acc, *lt_) + got_low)
            put(acc, *ut_, tile(acc, *ut_) + got_up)
        if last:
            advance(step, slice(16, 24), whole)
            advance(step, slice(24, 32), slice(0, 128))
            advance(step, slice(96, 104), slice(128, 256))
            advance(step, slice(104, 112), whole)
            fill_shares((0, lay.ny - 1))
        else:
            advance(step, lower, whole)
            advance(step, upper, whole)
            weigh((y1, y2)[step], lower)
            weigh((y1, y2)[step], upper)
            gather(RIM_HI, False)

    def wait_bytes(ref, send, slot):
        sem = (gram_send if send else gram_recv).at[slot]
        pltpu.make_async_copy(ref, ref, sem).wait()

    got[band] = shares[my_y]
    wait_bytes(got.at[0 : n_band - 1], False, 0)
    columns = got[...].astype(F32).reshape(8 * n_band, 128 * lay.per).astype(BF16)
    rows = jnp.concatenate(
        [got[y * lay.nz + my_z].astype(F32) for y in range(lay.ny)], axis=0
    ).astype(BF16)
    part[...] = dot_t(rows, columns).reshape(lay.ny, 8, 8 * n_band)

    def reduce(peers, src, dst, slot, index, own):
        for device, piece in peers:
            pltpu.make_async_remote_copy(
                src_ref=src(piece), dst_ref=dst.at[index],
                send_sem=gram_send.at[slot], recv_sem=gram_recv.at[slot],
                device_id=device, device_id_type=MESH,
            ).start()
        dst[index] = own
        wait_bytes(dst.at[0 : len(peers)], False, slot)
        total = dst[0]
        for i in range(1, len(peers) + 1):
            total = total + dst[i]
        return total

    y_peers = [lax.rem(my_y + i, lay.ny) for i in range(1, lay.ny)]
    sum1[...] = reduce(
        [((y * lay.nz + my_z, dom), y) for y in y_peers],
        lambda piece: part.at[piece], part_in, 1, my_y, part[my_y],
    )
    sum2[...] = reduce(
        [((band, peer), None) for peer in x_peers], lambda piece: sum1, sum1_in, 2, my_x, sum1[...]
    )
    total = reduce(
        [((band, peer), None) for peer in h_peers], lambda piece: sum2, sum2_in, 3, my_h, sum2[...]
    )
    gram[...] = total * (1.0 / nodes_all)

    for copy in started:
        copy.wait_send()
    wait_bytes(got.at[0 : n_band - 1], True, 0)
    wait_bytes(part_in.at[0 : lay.ny - 1], True, 1)
    wait_bytes(sum1_in.at[0 : lay.nx - 1], True, 2)
    wait_bytes(sum2_in.at[0 : lay.nh - 1], True, 3)


def local(lay, states_in, cell_nodes, cell_scale, cell_matrix, node_scale, potential):
    owned = states_in.shape[1]
    cells = cell_nodes.shape[0] * 384
    vmem, smem = pl.BlockSpec(memory_space=pltpu.VMEM), pl.BlockSpec(memory_space=pltpu.SMEM)
    n_band, share = lay.n_band, 128 * lay.per
    return pl.pallas_call(
        functools.partial(kernel, lay, owned * lay.n_dom),
        out_shape=(
            jax.ShapeDtypeStruct((8, owned), BF16),
            jax.ShapeDtypeStruct((8, 8 * n_band), F32),
        ),
        in_specs=[vmem, vmem, smem, vmem, vmem, vmem],
        out_specs=(vmem, vmem),
        scratch_shapes=[
            pltpu.VMEM((256, cells), BF16),
            pltpu.VMEM((cells, 256), BF16),
            pltpu.VMEM((384, 384), BF16),
            pltpu.VMEM((128, 384), jnp.int32),
            pltpu.VMEM((8, 8, 768), jnp.int32),
            pltpu.VMEM((128, 256), F32),
            pltpu.VMEM((128, 256), F32),
            pltpu.VMEM((128, 256), F32),
            pltpu.VMEM((128, 256), F32),
            pltpu.VMEM((128, 256), F32),
            pltpu.VMEM((128, 256), F32),
            pltpu.VMEM((128, 256), BF16),
            pltpu.VMEM((8, cells), F32),
            pltpu.VMEM((128, 384), BF16),
            pltpu.VMEM((16, cells), F32),
            pltpu.VMEM((128, cells), BF16),
            pltpu.VMEM((2, 16, 384), F32),
            pltpu.VMEM((2, 16, 384), F32),
            pltpu.VMEM((3, 48, 128), F32),
            pltpu.VMEM((3, 48, 128), F32),
            pltpu.VMEM((3, 48, 128), F32),
            pltpu.VMEM((3, 48, 128), F32),
            pltpu.VMEM((lay.ny, 8, share), BF16),
            pltpu.VMEM((n_band, 8, share), BF16),
            pltpu.VMEM((lay.ny, 8, 8 * n_band), F32),
            pltpu.VMEM((lay.ny, 8, 8 * n_band), F32),
            pltpu.VMEM((8, 8 * n_band), F32),
            pltpu.VMEM((lay.nx, 8, 8 * n_band), F32),
            pltpu.VMEM((8, 8 * n_band), F32),
            pltpu.VMEM((lay.nh, 8, 8 * n_band), F32),
            pltpu.SemaphoreType.DMA((8,)),
            pltpu.SemaphoreType.DMA((8,)),
            pltpu.SemaphoreType.DMA((4,)),
            pltpu.SemaphoreType.DMA((4,)),
        ],
        compiler_params=pltpu.CompilerParams(
            collective_id=0, has_side_effects=True, vmem_limit_bytes=48 * 1024 * 1024
        ),
    )(states_in, cell_nodes, cell_scale, cell_matrix, node_scale[None, :], potential[None, :])


def solution(mesh):
    lay = Layout(mesh.shape["band"], mesh.shape["dom"])
    in_specs = (P("band", "dom"), P("dom", None), P("dom"), P(), P("dom"), P("dom"))
    out_specs = (P("band", "dom"), P("band", None))
    return jax.shard_map(
        functools.partial(local, lay), mesh=mesh, in_specs=in_specs, out_specs=out_specs, check_vma=False
    )
```

```python
import functools

import jax
import jax.numpy as jnp
from jax import lax
from jax.experimental import pallas as pl
from jax.experimental.pallas import tpu as pltpu
from jax.sharding import PartitionSpec as P

CENTER = 0.25
HALF = 1.5
MESH = pl.DeviceIdType.MESH
F32 = jnp.float32
BF16 = jnp.bfloat16

RIM_HI = (0, 1, 2, 3, 12, 13, 14, 15)
MID_HI = (4, 5, 6, 7, 8, 9, 10, 11)
LOW_TILES = ((0, 1), (1, 0), (1, 1), (2, 0), (2, 1), (3, 0))
UP_TILES = ((12, 1), (13, 0), (13, 1), (14, 0), (14, 1), (15, 0))
OWN_TILES = tuple((2 + t // 2, t % 2) for t in range(24))


def tile(ref, hi, half):
    return ref[8 * hi : 8 * hi + 8, 128 * half : 128 * half + 128]


def put(ref, hi, half, value):
    ref[8 * hi : 8 * hi + 8, 128 * half : 128 * half + 128] = value


def dot_t(a, b):
    return lax.dot_general(a, b, (((1,), (1,)), ((), ())), preferred_element_type=F32)


class Layout:
    def __init__(self, n_band, n_dom):
        self.n_band, self.n_dom = n_band, n_dom
        self.ny, self.nz = 8, n_band // 8


def kernel(
    lay, nodes_all,
    states_hbm, nodes_hbm, scale_hbm, matrix_hbm, node_scale_hbm, potential_hbm,
    filtered_hbm, gram_hbm,
    filtered, gram, states, nodes, cell_scale, matrix, node_scale, potential,
    lt, le, mat, pad_nodes, hb, y0, y1, y2, ns, pc, acc, w2, mid, picked, x16, vh,
    stage, init_in, out_low, out_up, in_low, in_up, shares, got, got_edge, part, part_in, sums, sums_in,
    send_sem, recv_sem, gram_send, gram_recv, load_sem, store_sem,
):
    band, dom = lax.axis_index("band"), lax.axis_index("dom")
    n_band, n_dom = lay.n_band, lay.n_dom
    left, right = lax.rem(dom + n_dom - 1, n_dom), lax.rem(dom + 1, n_dom)
    my_y, my_z = band // lay.nz, lax.rem(band, lay.nz)
    has_left, has_right = dom > 0, dom < n_dom - 1
    odd = lax.rem(dom, 2)

    loads = [
        pltpu.make_async_copy(src, dst, load_sem.at[i])
        for i, (src, dst) in enumerate((
            (nodes_hbm, nodes), (matrix_hbm, matrix), (states_hbm, states),
            (node_scale_hbm, node_scale), (potential_hbm, potential), (scale_hbm, cell_scale),
        ))
    ]
    for load in loads:
        load.start()

    band_peers = [lax.rem(band + i, n_band) for i in range(1, n_band)]
    dom_peers = [lax.rem(dom + i, n_dom) for i in range(1, n_dom)]
    barrier = pltpu.get_barrier_semaphore()
    for peer in dom_peers:
        pl.semaphore_signal(barrier, inc=1, device_id=(band, peer), device_id_type=MESH)
    for peer in band_peers:
        pl.semaphore_signal(barrier, inc=1, device_id=(peer, dom), device_id_type=MESH)
    for load in loads:
        load.wait()

    pad_nodes[...] = jnp.full(pad_nodes.shape, -4096, jnp.int32)
    pad_nodes[:16, :343] = nodes[...]
    mat[...] = jnp.zeros(mat.shape, BF16)
    mat[:343, :343] = matrix[...]
    mat[...] = mat[...].astype(F32).T.astype(BF16)
    shifted = pad_nodes[...] + 128
    lo_all = shifted & 255
    hi_all = shifted >> 8
    lo_t = lo_all.T
    row_iota = lax.broadcasted_iota(jnp.int32, (256, 768), 0)
    lane_iota = lax.broadcasted_iota(jnp.int32, (384, 256), 1)
    for p in range(8):
        cols = slice(768 * p, 768 * p + 768)
        lo = jnp.concatenate([lo_all[2 * p : 2 * p + 1], lo_all[2 * p + 1 : 2 * p + 2]], axis=1)
        hi = jnp.concatenate([hi_all[2 * p : 2 * p + 1], hi_all[2 * p + 1 : 2 * p + 2]], axis=1)
        hb[p] = jnp.broadcast_to(hi, (8, 768))
        lt[:, cols] = jnp.where(row_iota == lo, 1.0, 0.0).astype(BF16)
        for c in (2 * p, 2 * p + 1):
            le[384 * c : 384 * c + 384, :] = jnp.where(
                lane_iota == lo_t[:, c : c + 1], 1.0, 0.0
            ).astype(BF16)

    for ref in (y0, ns, pc):
        ref[0:16] = jnp.zeros((16, 256), F32)
        ref[112:128] = jnp.zeros((16, 256), F32)
    for b in range(12):
        rows, cols = slice(16 + 8 * b, 24 + 8 * b), slice(256 * b, 256 * b + 256)
        y0[rows] = states[:, cols]
        ns[rows] = jnp.broadcast_to(node_scale[:, cols], (8, 256))
        pc[rows] = jnp.broadcast_to(potential[:, cols] - CENTER, (8, 256))
    for side, cols in ((0, slice(0, 384)), (1, slice(2688, 3072))):
        stage[side, 0:8] = states[:, cols]
        stage[side, 8:16] = jnp.concatenate(
            [node_scale[:, cols], potential[:, cols], jnp.zeros((6, 384), F32)], axis=0
        )

    pl.semaphore_wait(barrier, len(dom_peers) + len(band_peers))

    def rim_copy(src, dst, slot, to):
        copy = pltpu.make_async_remote_copy(
            src_ref=src, dst_ref=dst, send_sem=send_sem.at[slot], recv_sem=recv_sem.at[slot],
            device_id=(band, to), device_id_type=MESH,
        )
        copy.start()
        return copy

    started = [
        rim_copy(stage.at[0], init_in.at[1], 0, left),
        rim_copy(stage.at[1], init_in.at[0], 1, right),
    ]

    def gather(his, first):
        runs = [(his[0], his[-1] + 1)] if his == MID_HI else [(0, 4), (12, 16)]
        left_side = jnp.concatenate([w2[8 * a : 8 * b, :] for a, b in runs], axis=0)
        for p in range(8):
            cols = slice(768 * p, 768 * p + 768)
            t = jnp.dot(left_side, lt[:, cols], preferred_element_type=F32)
            index = hb[p]
            total = jnp.zeros((8, 768), F32) if first else mid[:, cols]
            for k, hi in enumerate(his):
                total = jnp.where(index == hi, t[8 * k : 8 * k + 8], total)
            if first:
                mid[:, cols] = total
            else:
                picked[16 * p : 16 * p + 16, :] = jnp.concatenate(
                    [total[:, :384], total[:, 384:]], axis=0
                ).astype(BF16)

    def scatter(his):
        for p in range(8):
            cols = slice(768 * p, 768 * p + 768)
            index = jnp.concatenate([hb[p], hb[p]], axis=0)
            x = x16[:, cols]
            for k, hi in enumerate(his):
                vh[16 * k : 16 * k + 16, cols] = jnp.where(index == hi, x, 0.0).astype(BF16)
        r = jnp.dot(vh[...], le[...], preferred_element_type=F32)
        for k, hi in enumerate(his):
            acc[8 * hi : 8 * hi + 8, :] = r[16 * k : 16 * k + 8] + r[16 * k + 8 : 16 * k + 16]

    def weigh(y, rows):
        w2[rows, :] = (ns[rows, :] * y[rows, :]).astype(BF16)

    def advance(step, rows, cols):
        now = (y0, y1, y2)[step][rows, cols]
        h = ns[rows, cols] * acc[rows, cols] + pc[rows, cols] * now
        if step == 0:
            y1[rows, cols] = h * (1.0 / HALF)
        elif step == 1:
            y2[rows, cols] = h * (2.0 / HALF) - y0[rows, cols]
        else:
            y1[rows, cols] = h * (2.0 / HALF) - y1[rows, cols]

    whole = slice(0, 256)
    middle, lower, upper = slice(32, 96), slice(0, 32), slice(96, 128)

    weigh(y0, middle)
    gather(MID_HI, True)
    for copy in started:
        copy.wait_recv()
    for side, tiles in ((0, LOW_TILES[:3]), (1, UP_TILES[3:])):
        there = has_left if side == 0 else has_right
        value = jnp.where(there, init_in[side], 0.0)
        for i, (hi, half) in enumerate(tiles):
            cols = slice(128 * i, 128 * i + 128)
            put(y0, hi, half, value[0:8, cols])
            put(ns, hi, half, jnp.broadcast_to(value[8:9, cols], (8, 128)))
            put(pc, hi, half, jnp.broadcast_to(value[9:10, cols] - CENTER, (8, 128)))
    weigh(y0, lower)
    weigh(y0, upper)
    gather(RIM_HI, False)

    outer = 7 * odd

    def gram_copy(src, dst, slot, device):
        pltpu.make_async_remote_copy(
            src_ref=src, dst_ref=dst, send_sem=gram_send.at[slot], recv_sem=gram_recv.at[slot],
            device_id=device, device_id_type=MESH,
        ).start()

    def wait_bytes(ref, send, slot):
        sem = (gram_send if send else gram_recv).at[slot]
        pltpu.make_async_copy(ref, ref, sem).wait()

    def send_share(share):
        for z in range(lay.nz):
            to = share * lay.nz + z

            @pl.when(band != to)
            def _():
                gram_copy(shares.at[share], got.at[band], 0, (to, dom))

    def fill_share(share):
        tiles = OWN_TILES[3 * share : 3 * share + 3]
        value = jnp.concatenate([tile(y1, *t) for t in tiles], axis=1).astype(BF16)
        shares[share] = value
        filtered[:, 384 * share : 384 * share + 384] = value

    def finish_edge(copy, low):
        copy.wait_recv()
        there, source = (has_left, in_low) if low else (has_right, in_up)
        for i, t in enumerate(LOW_TILES[3:] if low else UP_TILES[:3]):
            put(acc, *t, tile(acc, *t) + jnp.where(there, source[2, 8 * i : 8 * i + 8], 0.0))
        if low:
            advance(2, slice(16, 24), whole)
            advance(2, slice(24, 32), slice(0, 128))
        else:
            advance(2, slice(96, 104), slice(128, 256))
            advance(2, slice(104, 112), whole)
        fill_share(0 if low else 7)

    for step in range(3):
        cells = jnp.dot(picked[...], mat[...], preferred_element_type=F32)
        for p in range(8):
            x = jnp.concatenate(
                [cells[16 * p : 16 * p + 8] * cell_scale[2 * p],
                 cells[16 * p + 8 : 16 * p + 16] * cell_scale[2 * p + 1]], axis=1)
            rest = x - x.astype(BF16).astype(F32)
            x16[:, 768 * p : 768 * p + 768] = jnp.concatenate([x, rest], axis=0)
        scatter(RIM_HI)
        last = step == 2
        low_tiles, up_tiles = (LOW_TILES[:3], UP_TILES[3:]) if last else (LOW_TILES, UP_TILES)
        for i, (lt_, ut_) in enumerate(zip(low_tiles, up_tiles)):
            out_low[step, 8 * i : 8 * i + 8] = tile(acc, *lt_)
            out_up[step, 8 * i : 8 * i + 8] = tile(acc, *ut_)
        rows = 8 * len(low_tiles)
        now = [
            rim_copy(out_low.at[step, 0:rows], in_up.at[step, 0:rows], 2 + 2 * step, left),
            rim_copy(out_up.at[step, 0:rows], in_low.at[step, 0:rows], 3 + 2 * step, right),
        ]
        started += now
        scatter(MID_HI)
        advance(step, middle, whole)
        if last:
            advance(step, slice(24, 32), slice(128, 256))
            advance(step, slice(96, 104), slice(0, 128))
            for share in range(1, 7):
                fill_share(share)
            for i in range(6):
                send_share(1 + i)
            pl.when(odd == 1)(lambda: finish_edge(now[1], True))
            pl.when(odd == 0)(lambda: finish_edge(now[0], False))
            send_share(7 - outer)
            pl.when(odd == 1)(lambda: finish_edge(now[0], False))
            pl.when(odd == 0)(lambda: finish_edge(now[1], True))
            for peer in band_peers:
                gram_copy(shares.at[outer], got_edge.at[band], 1, (peer, dom))
            store = pltpu.make_async_copy(filtered, filtered_hbm, store_sem.at[0])
            store.start()
            continue
        weigh((y1, y2)[step], middle)
        gather(MID_HI, True)
        for copy in now:
            copy.wait_recv()
        for i, (lt_, ut_) in enumerate(zip(LOW_TILES, UP_TILES)):
            got_low = jnp.where(has_left, in_low[step, 8 * i : 8 * i + 8], 0.0)
            got_up = jnp.where(has_right, in_up[step, 8 * i : 8 * i + 8], 0.0)
            put(acc, *lt_, tile(acc, *lt_) + got_low)
            put(acc, *ut_, tile(acc, *ut_) + got_up)
        advance(step, lower, whole)
        advance(step, upper, whole)
        weigh((y1, y2)[step], lower)
        weigh((y1, y2)[step], upper)
        gather(RIM_HI, False)

    def stack(refs):
        return jnp.concatenate([ref.astype(F32) for ref in refs], axis=0).astype(BF16)

    @pl.when(my_y != outer)
    def _():
        got[band] = shares[my_y]
        wait_bytes(got.at[0 : n_band - 1], False, 0)
        columns = got[...].astype(F32).reshape(8 * n_band, 384).astype(BF16)
        rows = stack([got[y * lay.nz + my_z] for y in range(lay.ny)])
        part[...] = dot_t(rows, columns).reshape(lay.ny, 8, 8 * n_band)
        for i in range(1, lay.ny):
            y = lax.rem(my_y + i, lay.ny)
            gram_copy(part.at[y], part_in.at[my_y], 2, (y * lay.nz + my_z, dom))
        part_in[my_y] = part[my_y]
        part_in[outer] = jnp.zeros((8, 8 * n_band), F32)
        wait_bytes(part_in.at[0 : lay.ny - 2], False, 2)

    @pl.when(my_y == outer)
    def _():
        part_in[outer] = jnp.zeros((8, 8 * n_band), F32)
        wait_bytes(part_in.at[0 : lay.ny - 1], False, 2)

    total = part_in[0]
    for i in range(1, lay.ny):
        total = total + part_in[i]

    got_edge[band] = shares[outer]
    wait_bytes(got_edge.at[0 : n_band - 1], False, 1)
    columns = got_edge[...].astype(F32).reshape(8 * n_band, 384).astype(BF16)
    sums[...] = total + dot_t(shares[outer], columns)

    for peer in dom_peers:
        gram_copy(sums, sums_in.at[dom], 3, (band, peer))
    sums_in[dom] = sums[...]
    wait_bytes(sums_in.at[0 : n_dom - 1], False, 3)
    total = sums_in[0]
    for i in range(1, n_dom):
        total = total + sums_in[i]
    gram[...] = total * (1.0 / nodes_all)
    store_gram = pltpu.make_async_copy(gram, gram_hbm, store_sem.at[1])
    store_gram.start()

    for copy in started:
        copy.wait_send()

    @pl.when(my_y != outer)
    def _():
        wait_bytes(got.at[0 : 7 * lay.nz - 1], True, 0)
        wait_bytes(part_in.at[0 : lay.ny - 1], True, 2)

    @pl.when(my_y == outer)
    def _():
        wait_bytes(got.at[0 : 7 * lay.nz], True, 0)

    wait_bytes(got_edge.at[0 : n_band - 1], True, 1)
    wait_bytes(sums_in.at[0 : n_dom - 1], True, 3)
    store.wait()
    store_gram.wait()


def local(lay, states_in, cell_nodes, cell_scale, cell_matrix, node_scale, potential):
    owned = states_in.shape[1]
    cells = cell_nodes.shape[0] * 384
    hbm = pl.BlockSpec(memory_space=pltpu.HBM)
    n_band = lay.n_band
    return pl.pallas_call(
        functools.partial(kernel, lay, owned * lay.n_dom),
        out_shape=(
            jax.ShapeDtypeStruct((8, owned), BF16),
            jax.ShapeDtypeStruct((8, 8 * n_band), F32),
        ),
        in_specs=[hbm] * 6,
        out_specs=(hbm, hbm),
        scratch_shapes=[
            pltpu.VMEM((8, owned), BF16),
            pltpu.VMEM((8, 8 * n_band), F32),
            pltpu.VMEM(states_in.shape, F32),
            pltpu.VMEM(cell_nodes.shape, jnp.int32),
            pltpu.SMEM(cell_scale.shape, F32),
            pltpu.VMEM(cell_matrix.shape, BF16),
            pltpu.VMEM((1, owned), F32),
            pltpu.VMEM((1, owned), F32),
            pltpu.VMEM((256, cells), BF16),
            pltpu.VMEM((cells, 256), BF16),
            pltpu.VMEM((384, 384), BF16),
            pltpu.VMEM((128, 384), jnp.int32),
            pltpu.VMEM((8, 8, 768), jnp.int32),
            pltpu.VMEM((128, 256), F32),
            pltpu.VMEM((128, 256), F32),
            pltpu.VMEM((128, 256), F32),
            pltpu.VMEM((128, 256), F32),
            pltpu.VMEM((128, 256), F32),
            pltpu.VMEM((128, 256), F32),
            pltpu.VMEM((128, 256), BF16),
            pltpu.VMEM((8, cells), F32),
            pltpu.VMEM((128, 384), BF16),
            pltpu.VMEM((16, cells), F32),
            pltpu.VMEM((128, cells), BF16),
            pltpu.VMEM((2, 16, 384), F32),
            pltpu.VMEM((2, 16, 384), F32),
            pltpu.VMEM((3, 48, 128), F32),
            pltpu.VMEM((3, 48, 128), F32),
            pltpu.VMEM((3, 48, 128), F32),
            pltpu.VMEM((3, 48, 128), F32),
            pltpu.VMEM((8, 8, 384), BF16),
            pltpu.VMEM((n_band, 8, 384), BF16),
            pltpu.VMEM((n_band, 8, 384), BF16),
            pltpu.VMEM((lay.ny, 8, 8 * n_band), F32),
            pltpu.VMEM((lay.ny, 8, 8 * n_band), F32),
            pltpu.VMEM((8, 8 * n_band), F32),
            pltpu.VMEM((lay.n_dom, 8, 8 * n_band), F32),
            pltpu.SemaphoreType.DMA((8,)),
            pltpu.SemaphoreType.DMA((8,)),
            pltpu.SemaphoreType.DMA((4,)),
            pltpu.SemaphoreType.DMA((4,)),
            pltpu.SemaphoreType.DMA((6,)),
            pltpu.SemaphoreType.DMA((2,)),
        ],
        compiler_params=pltpu.CompilerParams(
            collective_id=0, has_side_effects=True, vmem_limit_bytes=60 * 1024 * 1024
        ),
    )(states_in, cell_nodes, cell_scale, cell_matrix, node_scale[None, :], potential[None, :])


def solution(mesh):
    lay = Layout(mesh.shape["band"], mesh.shape["dom"])
    in_specs = (P("band", "dom"), P("dom", None), P("dom"), P(), P("dom"), P("dom"))
    out_specs = (P("band", "dom"), P("band", None))
    return jax.shard_map(
        functools.partial(local, lay), mesh=mesh, in_specs=in_specs, out_specs=out_specs, check_vma=False
    )
```

```python
import functools

import jax
import jax.numpy as jnp
from jax import lax
from jax.experimental import pallas as pl
from jax.experimental.pallas import tpu as pltpu
from jax.sharding import PartitionSpec as P

CENTER = 0.25
HALF = 1.5
MESH = pl.DeviceIdType.MESH
F32 = jnp.float32
BF16 = jnp.bfloat16

RIM_HI = (0, 1, 2, 3, 12, 13, 14, 15)
RIM_TILES = tuple((t // 2, t % 2) for t in (*range(1, 8), *range(24, 31)))
MID_HI = (4, 5, 6, 7, 8, 9, 10, 11)
LOW_TILES = ((0, 1), (1, 0), (1, 1), (2, 0), (2, 1), (3, 0))
UP_TILES = ((12, 1), (13, 0), (13, 1), (14, 0), (14, 1), (15, 0))
OWN_TILES = tuple((2 + t // 2, t % 2) for t in range(24))


def tile(ref, hi, half):
    return ref[8 * hi : 8 * hi + 8, 128 * half : 128 * half + 128]


def put(ref, hi, half, value):
    ref[8 * hi : 8 * hi + 8, 128 * half : 128 * half + 128] = value


def dot_t(a, b):
    return lax.dot_general(a, b, (((1,), (1,)), ((), ())), preferred_element_type=F32)


class Layout:
    def __init__(self, n_band, n_dom):
        self.n_band, self.n_dom = n_band, n_dom
        self.ny, self.nz = 8, n_band // 8


def kernel(
    lay, nodes_all,
    states_hbm, nodes_hbm, scale_hbm, matrix_hbm, node_scale_hbm, potential_hbm,
    filtered_hbm, gram_hbm,
    filtered, gram, states, nodes, cell_scale, matrix, node_scale, potential,
    lt, lt_half, le, mat, pad_nodes, hb, hb_half, y0, y1, y2, ns, pc, acc, w1, w2, mid, x16, vh,
    stage, init_in, out_low, out_up, in_low, in_up, shares, got, got_edge, part, part_in, sums, sums_in,
    send_sem, recv_sem, gram_send, gram_recv, load_sem, store_sem,
):
    band, dom = lax.axis_index("band"), lax.axis_index("dom")
    n_band, n_dom = lay.n_band, lay.n_dom
    left, right = lax.rem(dom + n_dom - 1, n_dom), lax.rem(dom + 1, n_dom)
    my_y, my_z = band // lay.nz, lax.rem(band, lay.nz)
    has_left, has_right = dom > 0, dom < n_dom - 1
    odd = lax.rem(dom, 2)

    band_peers = [lax.rem(band + i, n_band) for i in range(1, n_band)]
    order = [i for i in (n_dom - 1, *range(1, n_dom - 1))]
    dom_peers = [lax.rem(dom + i, n_dom) for i in order]
    barrier = pltpu.get_barrier_semaphore()
    for peer in dom_peers:
        pl.semaphore_signal(barrier, inc=1, device_id=(band, peer), device_id_type=MESH)
    for peer in band_peers:
        pl.semaphore_signal(barrier, inc=1, device_id=(peer, dom), device_id_type=MESH)
    loads = [
        pltpu.make_async_copy(src, dst, load_sem.at[i])
        for i, (src, dst) in enumerate((
            (nodes_hbm, nodes), (matrix_hbm, matrix), (states_hbm, states),
            (node_scale_hbm, node_scale), (potential_hbm, potential), (scale_hbm, cell_scale),
        ))
    ]
    for load in loads:
        load.start()
    for load in loads:
        load.wait()

    pad_nodes[...] = jnp.full(pad_nodes.shape, -4096, jnp.int32)
    pad_nodes[:16, :343] = nodes[...]
    mat[...] = jnp.zeros(mat.shape, BF16)
    mat[:343, :343] = matrix[...]
    mat[...] = mat[...].astype(F32).T.astype(BF16)
    shifted = pad_nodes[...] + 128
    lo_all = shifted & 255
    hi_all = shifted >> 8
    lo_t = lo_all.T
    row_iota = lax.broadcasted_iota(jnp.int32, (256, 768), 0)
    lane_iota = lax.broadcasted_iota(jnp.int32, (384, 256), 1)
    for p in range(8):
        cols = slice(768 * p, 768 * p + 768)
        lo = jnp.concatenate([lo_all[2 * p : 2 * p + 1], lo_all[2 * p + 1 : 2 * p + 2]], axis=1)
        hi = jnp.concatenate([hi_all[2 * p : 2 * p + 1], hi_all[2 * p + 1 : 2 * p + 2]], axis=1)
        hb[p] = jnp.broadcast_to(hi, (8, 768))
        hb_half[p] = jnp.broadcast_to(2 * hi + (lo >> 7), (8, 768))
        lt[:, cols] = jnp.where(row_iota == lo, 1.0, 0.0).astype(BF16)
        lt_half[:, cols] = jnp.where(row_iota[:128] == (lo & 127), 1.0, 0.0).astype(BF16)
        for c in (2 * p, 2 * p + 1):
            le[384 * c : 384 * c + 384, :] = jnp.where(
                lane_iota == lo_t[:, c : c + 1], 1.0, 0.0
            ).astype(BF16)

    for ref in (y0, ns, pc):
        ref[0:16] = jnp.zeros((16, 256), F32)
        ref[112:128] = jnp.zeros((16, 256), F32)
    for b in range(12):
        rows, cols = slice(16 + 8 * b, 24 + 8 * b), slice(256 * b, 256 * b + 256)
        y0[rows] = states[:, cols]
        ns[rows] = jnp.broadcast_to(node_scale[:, cols], (8, 256))
        pc[rows] = jnp.broadcast_to(potential[:, cols] - CENTER, (8, 256))
    for side, cols in ((0, slice(0, 384)), (1, slice(2688, 3072))):
        stage[side, 0:8] = states[:, cols]
        stage[side, 8:16] = jnp.concatenate(
            [node_scale[:, cols], potential[:, cols], jnp.zeros((6, 384), F32)], axis=0
        )

    pl.semaphore_wait(barrier, len(dom_peers) + len(band_peers))

    def rim_copy(src, dst, slot, to):
        copy = pltpu.make_async_remote_copy(
            src_ref=src, dst_ref=dst, send_sem=send_sem.at[slot], recv_sem=recv_sem.at[slot],
            device_id=(band, to), device_id_type=MESH,
        )
        copy.start()
        return copy

    started = [
        rim_copy(stage.at[0], init_in.at[1], 0, left),
        rim_copy(stage.at[1], init_in.at[0], 1, right),
    ]

    def gather_mid():
        for p in range(8):
            cols = slice(768 * p, 768 * p + 768)
            t = jnp.dot(w2[...], lt[:, cols], preferred_element_type=F32)
            index = hb[p]
            total = jnp.zeros((8, 768), F32)
            for k, hi in enumerate(MID_HI):
                total = jnp.where(index == hi, t[8 * k : 8 * k + 8], total)
            mid[:, cols] = total

    def gather_rim(p):
        cols = slice(768 * p, 768 * p + 768)
        t = jnp.dot(w1[...], lt_half[:, cols], preferred_element_type=F32)
        index = hb_half[p]
        total = mid[:, cols]
        for k, (hi, half) in enumerate(RIM_TILES):
            total = jnp.where(index == 2 * hi + half, t[8 * k : 8 * k + 8], total)
        return [total[:, :384], total[:, 384:]]

    def spread(his, p, x):
        cols = slice(768 * p, 768 * p + 768)
        index = jnp.concatenate([hb[p], hb[p]], axis=0)
        for k, hi in enumerate(his):
            vh[16 * k : 16 * k + 16, cols] = jnp.where(index == hi, x, 0.0).astype(BF16)

    def collect(his, r):
        for k, hi in enumerate(his):
            acc[8 * hi : 8 * hi + 8, :] = r[16 * k : 16 * k + 8] + r[16 * k + 8 : 16 * k + 16]

    def rim_pass():
        values = jnp.concatenate([v for p in range(8) for v in gather_rim(p)], axis=0).astype(BF16)
        cells = jnp.dot(values, mat[...], preferred_element_type=F32)
        for p in range(8):
            x = jnp.concatenate(
                [cells[16 * p : 16 * p + 8] * cell_scale[2 * p],
                 cells[16 * p + 8 : 16 * p + 16] * cell_scale[2 * p + 1]], axis=1)
            x = jnp.concatenate([x, x - x.astype(BF16).astype(F32)], axis=0)
            x16[:, 768 * p : 768 * p + 768] = x
            spread(RIM_HI, p, x)
        collect(RIM_HI, jnp.dot(vh[...], le[...], preferred_element_type=F32))

    def scatter_mid():
        for p in range(8):
            spread(MID_HI, p, x16[:, 768 * p : 768 * p + 768])
        collect(MID_HI, jnp.dot(vh[...], le[...], preferred_element_type=F32))

    def weigh_mid(y):
        w2[...] = (ns[32:96] * y[32:96]).astype(BF16)

    def weigh_rim(y):
        for i in range(0, len(RIM_TILES), 2):
            pair = [tile(ns, *t) * tile(y, *t) for t in RIM_TILES[i : i + 2]]
            w1[8 * i : 8 * i + 16, :] = jnp.concatenate(pair, axis=0).astype(BF16)

    def advance(step, rows, cols):
        now = (y0, y1, y2)[step][rows, cols]
        h = ns[rows, cols] * acc[rows, cols] + pc[rows, cols] * now
        if step == 0:
            y1[rows, cols] = h * (1.0 / HALF)
        elif step == 1:
            y2[rows, cols] = h * (2.0 / HALF) - y0[rows, cols]
        else:
            y1[rows, cols] = h * (2.0 / HALF) - y1[rows, cols]

    whole = slice(0, 256)
    middle, lower, upper = slice(32, 96), slice(0, 32), slice(96, 128)

    weigh_mid(y0)
    gather_mid()
    for copy in started:
        copy.wait_recv()
    for side, tiles in ((0, LOW_TILES[:3]), (1, UP_TILES[3:])):
        there = has_left if side == 0 else has_right
        value = jnp.where(there, init_in[side], 0.0)
        for i, (hi, half) in enumerate(tiles):
            cols = slice(128 * i, 128 * i + 128)
            put(y0, hi, half, value[0:8, cols])
            put(ns, hi, half, jnp.broadcast_to(value[8:9, cols], (8, 128)))
            put(pc, hi, half, jnp.broadcast_to(value[9:10, cols] - CENTER, (8, 128)))
    weigh_rim(y0)

    outer = 7 * odd

    def gram_copy(src, dst, slot, device):
        pltpu.make_async_remote_copy(
            src_ref=src, dst_ref=dst, send_sem=gram_send.at[slot], recv_sem=gram_recv.at[slot],
            device_id=device, device_id_type=MESH,
        ).start()

    def wait_bytes(ref, send, slot):
        sem = (gram_send if send else gram_recv).at[slot]
        pltpu.make_async_copy(ref, ref, sem).wait()

    def send_share(share):
        for z in range(lay.nz):
            to = share * lay.nz + z

            @pl.when(band != to)
            def _():
                gram_copy(shares.at[share], got.at[band], 0, (to, dom))

    def fill_share(share):
        tiles = OWN_TILES[3 * share : 3 * share + 3]
        value = jnp.concatenate([tile(y1, *t) for t in tiles], axis=1).astype(BF16)
        shares[share] = value
        filtered[:, 384 * share : 384 * share + 384] = value

    def finish_edge(copy, low):
        copy.wait_recv()
        there, source = (has_left, in_low) if low else (has_right, in_up)
        for i, t in enumerate(LOW_TILES[3:] if low else UP_TILES[:3]):
            put(acc, *t, tile(acc, *t) + jnp.where(there, source[2, 8 * i : 8 * i + 8], 0.0))
        if low:
            advance(2, slice(16, 24), whole)
            advance(2, slice(24, 32), slice(0, 128))
        else:
            advance(2, slice(96, 104), slice(128, 256))
            advance(2, slice(104, 112), whole)
        fill_share(0 if low else 7)

    for step in range(3):
        rim_pass()
        last = step == 2
        low_tiles, up_tiles = (LOW_TILES[:3], UP_TILES[3:]) if last else (LOW_TILES, UP_TILES)
        for i, (lt_, ut_) in enumerate(zip(low_tiles, up_tiles)):
            out_low[step, 8 * i : 8 * i + 8] = tile(acc, *lt_)
            out_up[step, 8 * i : 8 * i + 8] = tile(acc, *ut_)
        rows = 8 * len(low_tiles)
        now = [
            rim_copy(out_low.at[step, 0:rows], in_up.at[step, 0:rows], 2 + 2 * step, left),
            rim_copy(out_up.at[step, 0:rows], in_low.at[step, 0:rows], 3 + 2 * step, right),
        ]
        started += now
        scatter_mid()
        advance(step, middle, whole)
        if last:
            advance(step, slice(24, 32), slice(128, 256))
            advance(step, slice(96, 104), slice(0, 128))
            for share in range(1, 7):
                fill_share(share)
            for i in range(6):
                send_share(1 + i)
            pl.when(odd == 1)(lambda: finish_edge(now[1], True))
            pl.when(odd == 0)(lambda: finish_edge(now[0], False))
            send_share(7 - outer)
            pl.when(odd == 1)(lambda: finish_edge(now[0], False))
            pl.when(odd == 0)(lambda: finish_edge(now[1], True))
            for peer in band_peers:
                gram_copy(shares.at[outer], got_edge.at[band], 1, (peer, dom))
            store = pltpu.make_async_copy(filtered, filtered_hbm, store_sem.at[0])
            store.start()
            continue
        weigh_mid((y1, y2)[step])
        gather_mid()
        for copy in now:
            copy.wait_recv()
        for i, (lt_, ut_) in enumerate(zip(LOW_TILES, UP_TILES)):
            got_low = jnp.where(has_left, in_low[step, 8 * i : 8 * i + 8], 0.0)
            got_up = jnp.where(has_right, in_up[step, 8 * i : 8 * i + 8], 0.0)
            put(acc, *lt_, tile(acc, *lt_) + got_low)
            put(acc, *ut_, tile(acc, *ut_) + got_up)
        advance(step, lower, whole)
        advance(step, upper, whole)
        weigh_rim((y1, y2)[step])

    def stack(refs):
        return jnp.concatenate([ref.astype(F32) for ref in refs], axis=0).astype(BF16)

    @pl.when(my_y != outer)
    def _():
        got[band] = shares[my_y]
        wait_bytes(got.at[0 : n_band - 1], False, 0)
        columns = got[...].astype(F32).reshape(8 * n_band, 384).astype(BF16)
        rows = stack([got[y * lay.nz + my_z] for y in range(lay.ny)])
        part[...] = dot_t(rows, columns).reshape(lay.ny, 8, 8 * n_band)
        for i in range(1, lay.ny):
            y = lax.rem(my_y + i, lay.ny)
            gram_copy(part.at[y], part_in.at[my_y], 2, (y * lay.nz + my_z, dom))
        part_in[my_y] = part[my_y]
        part_in[outer] = jnp.zeros((8, 8 * n_band), F32)
        wait_bytes(part_in.at[0 : lay.ny - 2], False, 2)

    @pl.when(my_y == outer)
    def _():
        part_in[outer] = jnp.zeros((8, 8 * n_band), F32)
        wait_bytes(part_in.at[0 : lay.ny - 1], False, 2)

    total = part_in[0]
    for i in range(1, lay.ny):
        total = total + part_in[i]

    got_edge[band] = shares[outer]
    wait_bytes(got_edge.at[0 : n_band - 1], False, 1)
    columns = got_edge[...].astype(F32).reshape(8 * n_band, 384).astype(BF16)
    sums[...] = (total + dot_t(shares[outer], columns)).astype(BF16)

    for peer in dom_peers:
        gram_copy(sums, sums_in.at[dom], 3, (band, peer))
    sums_in[dom] = sums[...]
    wait_bytes(sums_in.at[0 : n_dom - 1], False, 3)
    total = jnp.sum(sums_in[...].astype(F32), axis=0)
    gram[...] = total * (1.0 / nodes_all)
    store_gram = pltpu.make_async_copy(gram, gram_hbm, store_sem.at[1])
    store_gram.start()

    for copy in started:
        copy.wait_send()

    @pl.when(my_y != outer)
    def _():
        wait_bytes(got.at[0 : 7 * lay.nz - 1], True, 0)
        wait_bytes(part_in.at[0 : lay.ny - 1], True, 2)

    @pl.when(my_y == outer)
    def _():
        wait_bytes(got.at[0 : 7 * lay.nz], True, 0)

    wait_bytes(got_edge.at[0 : n_band - 1], True, 1)
    wait_bytes(sums_in.at[0 : n_dom - 1], True, 3)
    store.wait()
    store_gram.wait()


def hand_over(filtered_from, gram_from, filtered, gram, sem):
    copies = [
        pltpu.make_async_copy(filtered_from, filtered, sem.at[0]),
        pltpu.make_async_copy(gram_from, gram, sem.at[1]),
    ]
    for copy in copies:
        copy.start()
    for copy in copies:
        copy.wait()


def local(lay, states_in, cell_nodes, cell_scale, cell_matrix, node_scale, potential):
    owned = states_in.shape[1]
    cells = cell_nodes.shape[0] * 384
    hbm = pl.BlockSpec(memory_space=pltpu.HBM)
    n_band = lay.n_band
    out_shape = (
        jax.ShapeDtypeStruct((8, owned), BF16),
        jax.ShapeDtypeStruct((8, 8 * n_band), F32),
    )
    results = pl.pallas_call(
        functools.partial(kernel, lay, owned * lay.n_dom),
        out_shape=out_shape,
        in_specs=[hbm] * 6,
        out_specs=(hbm, hbm),
        scratch_shapes=[
            pltpu.VMEM((8, owned), BF16),
            pltpu.VMEM((8, 8 * n_band), F32),
            pltpu.VMEM(states_in.shape, F32),
            pltpu.VMEM(cell_nodes.shape, jnp.int32),
            pltpu.SMEM(cell_scale.shape, F32),
            pltpu.VMEM(cell_matrix.shape, BF16),
            pltpu.VMEM((1, owned), F32),
            pltpu.VMEM((1, owned), F32),
            pltpu.VMEM((256, cells), BF16),
            pltpu.VMEM((128, cells), BF16),
            pltpu.VMEM((cells, 256), BF16),
            pltpu.VMEM((384, 384), BF16),
            pltpu.VMEM((128, 384), jnp.int32),
            pltpu.VMEM((8, 8, 768), jnp.int32),
            pltpu.VMEM((8, 8, 768), jnp.int32),
            pltpu.VMEM((128, 256), F32),
            pltpu.VMEM((128, 256), F32),
            pltpu.VMEM((128, 256), F32),
            pltpu.VMEM((128, 256), F32),
            pltpu.VMEM((128, 256), F32),
            pltpu.VMEM((128, 256), F32),
            pltpu.VMEM((112, 128), BF16),
            pltpu.VMEM((64, 256), BF16),
            pltpu.VMEM((8, cells), F32),
            pltpu.VMEM((16, cells), F32),
            pltpu.VMEM((128, cells), BF16),
            pltpu.VMEM((2, 16, 384), F32),
            pltpu.VMEM((2, 16, 384), F32),
            pltpu.VMEM((3, 48, 128), F32),
            pltpu.VMEM((3, 48, 128), F32),
            pltpu.VMEM((3, 48, 128), F32),
            pltpu.VMEM((3, 48, 128), F32),
            pltpu.VMEM((8, 8, 384), BF16),
            pltpu.VMEM((n_band, 8, 384), BF16),
            pltpu.VMEM((n_band, 8, 384), BF16),
            pltpu.VMEM((lay.ny, 8, 8 * n_band), F32),
            pltpu.VMEM((lay.ny, 8, 8 * n_band), F32),
            pltpu.VMEM((8, 8 * n_band), BF16),
            pltpu.VMEM((lay.n_dom, 8, 8 * n_band), BF16),
            pltpu.SemaphoreType.DMA((8,)),
            pltpu.SemaphoreType.DMA((8,)),
            pltpu.SemaphoreType.DMA((4,)),
            pltpu.SemaphoreType.DMA((4,)),
            pltpu.SemaphoreType.DMA((6,)),
            pltpu.SemaphoreType.DMA((2,)),
        ],
        compiler_params=pltpu.CompilerParams(
            collective_id=0, has_side_effects=True, vmem_limit_bytes=60 * 1024 * 1024
        ),
    )(states_in, cell_nodes, cell_scale, cell_matrix, node_scale[None, :], potential[None, :])
    return pl.pallas_call(
        hand_over, out_shape=out_shape, in_specs=[hbm] * 2, out_specs=(hbm, hbm),
        scratch_shapes=[pltpu.SemaphoreType.DMA((2,))],
        compiler_params=pltpu.CompilerParams(vmem_limit_bytes=60 * 1024 * 1024),
    )(*results)


def solution(mesh):
    lay = Layout(mesh.shape["band"], mesh.shape["dom"])
    in_specs = (P("band", "dom"), P("dom", None), P("dom"), P(), P("dom"), P("dom"))
    out_specs = (P("band", "dom"), P("band", None))
    return jax.shard_map(
        functools.partial(local, lay), mesh=mesh, in_specs=in_specs, out_specs=out_specs, check_vma=False
    )
```

```python
import functools

import jax
import jax.numpy as jnp
from jax import lax
from jax.experimental import pallas as pl
from jax.experimental.pallas import tpu as pltpu
from jax.sharding import PartitionSpec as P

CENTER = 0.25
HALF = 1.5
MESH = pl.DeviceIdType.MESH
F32 = jnp.float32
BF16 = jnp.bfloat16

RIM_HI = (0, 1, 2, 3, 12, 13, 14, 15)
RIM_TILES = tuple((t // 2, t % 2) for t in (*range(1, 8), *range(24, 31)))
MID_HI = (4, 5, 6, 7, 8, 9, 10, 11)
LOW_TILES = ((0, 1), (1, 0), (1, 1), (2, 0), (2, 1), (3, 0))
UP_TILES = ((12, 1), (13, 0), (13, 1), (14, 0), (14, 1), (15, 0))
OWN_TILES = tuple((2 + t // 2, t % 2) for t in range(24))


def tile(ref, hi, half):
    return ref[8 * hi : 8 * hi + 8, 128 * half : 128 * half + 128]


def put(ref, hi, half, value):
    ref[8 * hi : 8 * hi + 8, 128 * half : 128 * half + 128] = value


def dot_t(a, b):
    return lax.dot_general(a, b, (((1,), (1,)), ((), ())), preferred_element_type=F32)


class Layout:
    def __init__(self, n_band, n_dom):
        self.n_band, self.n_dom = n_band, n_dom
        self.ny, self.nz = 8, n_band // 8


def kernel(
    lay, nodes_all,
    states_hbm, nodes_hbm, scale_hbm, matrix_hbm, node_scale_hbm, potential_hbm,
    filtered_hbm, gram_hbm,
    filtered, gram, states, nodes, cell_scale, matrix, node_scale, potential,
    lt, lt_half, le, mat, pad_nodes, hb, hb_half, y0, y1, y2, ns, pc, acc, w1, w2, mid, x16, vh,
    stage, init_in, out_low, out_up, in_low, in_up, shares, got, got_edge, part, part_in, sums, sums_in,
    send_sem, recv_sem, gram_send, gram_recv, load_sem, store_sem,
):
    band, dom = lax.axis_index("band"), lax.axis_index("dom")
    n_band, n_dom = lay.n_band, lay.n_dom
    left, right = lax.rem(dom + n_dom - 1, n_dom), lax.rem(dom + 1, n_dom)
    my_y, my_z = band // lay.nz, lax.rem(band, lay.nz)
    has_left, has_right = dom > 0, dom < n_dom - 1
    odd = lax.rem(dom, 2)

    band_peers = [
        lax.rem(my_y + dy, lay.ny) * lay.nz + lax.rem(my_z + dz, lay.nz)
        for dy in (4, 3, 5, 2, 6, 1, 7, 0) for dz in range(lay.nz) if dy or dz
    ]
    order = [i for i in (n_dom - 1, *range(1, n_dom - 1))]
    dom_peers = [lax.rem(dom + i, n_dom) for i in order]
    barrier = pltpu.get_barrier_semaphore()
    for peer in dom_peers:
        pl.semaphore_signal(barrier, inc=1, device_id=(band, peer), device_id_type=MESH)
    for peer in band_peers:
        pl.semaphore_signal(barrier, inc=1, device_id=(peer, dom), device_id_type=MESH)
    loads = [
        pltpu.make_async_copy(src, dst, load_sem.at[i])
        for i, (src, dst) in enumerate((
            (nodes_hbm, nodes), (matrix_hbm, matrix), (states_hbm, states),
            (node_scale_hbm, node_scale), (potential_hbm, potential), (scale_hbm, cell_scale),
        ))
    ]
    for load in loads:
        load.start()
    for load in loads:
        load.wait()

    pad_nodes[...] = jnp.full(pad_nodes.shape, -4096, jnp.int32)
    pad_nodes[:16, :343] = nodes[...]
    mat[...] = jnp.zeros(mat.shape, BF16)
    mat[:343, :343] = matrix[...]
    mat[...] = mat[...].astype(F32).T.astype(BF16)
    shifted = pad_nodes[...] + 128
    lo_all = shifted & 255
    hi_all = shifted >> 8
    lo_t = lo_all.T
    row_iota = lax.broadcasted_iota(jnp.int32, (256, 768), 0)
    lane_iota = lax.broadcasted_iota(jnp.int32, (384, 256), 1)
    for p in range(8):
        cols = slice(768 * p, 768 * p + 768)
        lo = jnp.concatenate([lo_all[2 * p : 2 * p + 1], lo_all[2 * p + 1 : 2 * p + 2]], axis=1)
        hi = jnp.concatenate([hi_all[2 * p : 2 * p + 1], hi_all[2 * p + 1 : 2 * p + 2]], axis=1)
        hb[p] = jnp.broadcast_to(hi, (8, 768))
        hb_half[p] = jnp.broadcast_to(2 * hi + (lo >> 7), (8, 768))
        lt[:, cols] = jnp.where(row_iota == lo, 1.0, 0.0).astype(BF16)
        lt_half[:, cols] = jnp.where(row_iota[:128] == (lo & 127), 1.0, 0.0).astype(BF16)
        for c in (2 * p, 2 * p + 1):
            le[384 * c : 384 * c + 384, :] = jnp.where(
                lane_iota == lo_t[:, c : c + 1], 1.0, 0.0
            ).astype(BF16)

    for ref in (y0, ns, pc):
        ref[0:16] = jnp.zeros((16, 256), F32)
        ref[112:128] = jnp.zeros((16, 256), F32)
    for b in range(12):
        rows, cols = slice(16 + 8 * b, 24 + 8 * b), slice(256 * b, 256 * b + 256)
        y0[rows] = states[:, cols]
        ns[rows] = jnp.broadcast_to(node_scale[:, cols], (8, 256))
        pc[rows] = jnp.broadcast_to(potential[:, cols] - CENTER, (8, 256))
    for side, cols in ((0, slice(0, 384)), (1, slice(2688, 3072))):
        stage[side, 0:8] = states[:, cols]
        stage[side, 8:16] = jnp.concatenate(
            [node_scale[:, cols], potential[:, cols], jnp.zeros((6, 384), F32)], axis=0
        )

    pl.semaphore_wait(barrier, len(dom_peers) + len(band_peers))

    def rim_copy(src, dst, slot, to):
        copy = pltpu.make_async_remote_copy(
            src_ref=src, dst_ref=dst, send_sem=send_sem.at[slot], recv_sem=recv_sem.at[slot],
            device_id=(band, to), device_id_type=MESH,
        )
        copy.start()
        return copy

    started = [
        rim_copy(stage.at[0], init_in.at[1], 0, left),
        rim_copy(stage.at[1], init_in.at[0], 1, right),
    ]

    def gather_mid():
        for p in range(8):
            cols = slice(768 * p, 768 * p + 768)
            t = jnp.dot(w2[...], lt[:, cols], preferred_element_type=F32)
            index = hb[p]
            total = jnp.zeros((8, 768), F32)
            for k, hi in enumerate(MID_HI):
                total = jnp.where(index == hi, t[8 * k : 8 * k + 8], total)
            mid[:, cols] = total

    def gather_rim(p):
        cols = slice(768 * p, 768 * p + 768)
        t = jnp.dot(w1[...], lt_half[:, cols], preferred_element_type=F32)
        index = hb_half[p]
        total = mid[:, cols]
        for k, (hi, half) in enumerate(RIM_TILES):
            total = jnp.where(index == 2 * hi + half, t[8 * k : 8 * k + 8], total)
        return [total[:, :384], total[:, 384:]]

    def spread(his, p, x):
        cols = slice(768 * p, 768 * p + 768)
        index = jnp.concatenate([hb[p], hb[p]], axis=0)
        for k, hi in enumerate(his):
            vh[16 * k : 16 * k + 16, cols] = jnp.where(index == hi, x, 0.0).astype(BF16)

    def collect(his, r):
        for k, hi in enumerate(his):
            acc[8 * hi : 8 * hi + 8, :] = r[16 * k : 16 * k + 8] + r[16 * k + 8 : 16 * k + 16]

    def rim_pass():
        values = jnp.concatenate([v for p in range(8) for v in gather_rim(p)], axis=0).astype(BF16)
        cells = jnp.dot(values, mat[...], preferred_element_type=F32)
        for p in range(8):
            x = jnp.concatenate(
                [cells[16 * p : 16 * p + 8] * cell_scale[2 * p],
                 cells[16 * p + 8 : 16 * p + 16] * cell_scale[2 * p + 1]], axis=1)
            x = jnp.concatenate([x, x - x.astype(BF16).astype(F32)], axis=0)
            x16[:, 768 * p : 768 * p + 768] = x
            spread(RIM_HI, p, x)
        collect(RIM_HI, jnp.dot(vh[...], le[...], preferred_element_type=F32))

    def scatter_mid():
        for p in range(8):
            spread(MID_HI, p, x16[:, 768 * p : 768 * p + 768])
        collect(MID_HI, jnp.dot(vh[...], le[...], preferred_element_type=F32))

    def weigh_mid(y):
        w2[...] = (ns[32:96] * y[32:96]).astype(BF16)

    def weigh_rim(y):
        for i in range(0, len(RIM_TILES), 2):
            pair = [tile(ns, *t) * tile(y, *t) for t in RIM_TILES[i : i + 2]]
            w1[8 * i : 8 * i + 16, :] = jnp.concatenate(pair, axis=0).astype(BF16)

    def advance(step, rows, cols):
        now = (y0, y1, y2)[step][rows, cols]
        h = ns[rows, cols] * acc[rows, cols] + pc[rows, cols] * now
        if step == 0:
            y1[rows, cols] = h * (1.0 / HALF)
        elif step == 1:
            y2[rows, cols] = h * (2.0 / HALF) - y0[rows, cols]
        else:
            y1[rows, cols] = h * (2.0 / HALF) - y1[rows, cols]

    whole = slice(0, 256)
    middle, lower, upper = slice(32, 96), slice(0, 32), slice(96, 128)

    weigh_mid(y0)
    gather_mid()
    for copy in started:
        copy.wait_recv()
    for side, tiles in ((0, LOW_TILES[:3]), (1, UP_TILES[3:])):
        there = has_left if side == 0 else has_right
        value = jnp.where(there, init_in[side], 0.0)
        for i, (hi, half) in enumerate(tiles):
            cols = slice(128 * i, 128 * i + 128)
            put(y0, hi, half, value[0:8, cols])
            put(ns, hi, half, jnp.broadcast_to(value[8:9, cols], (8, 128)))
            put(pc, hi, half, jnp.broadcast_to(value[9:10, cols] - CENTER, (8, 128)))
    weigh_rim(y0)

    outer = 7 * odd

    def gram_copy(src, dst, slot, device):
        pltpu.make_async_remote_copy(
            src_ref=src, dst_ref=dst, send_sem=gram_send.at[slot], recv_sem=gram_recv.at[slot],
            device_id=device, device_id_type=MESH,
        ).start()

    def wait_bytes(ref, send, slot):
        sem = (gram_send if send else gram_recv).at[slot]
        pltpu.make_async_copy(ref, ref, sem).wait()

    def send_share(share):
        for z in range(lay.nz):
            to = share * lay.nz + z

            @pl.when(band != to)
            def _():
                gram_copy(shares.at[share], got.at[band], 0, (to, dom))

    def fill_share(share):
        tiles = OWN_TILES[3 * share : 3 * share + 3]
        value = jnp.concatenate([tile(y1, *t) for t in tiles], axis=1).astype(BF16)
        shares[share] = value
        filtered[:, 384 * share : 384 * share + 384] = value

    def finish_edge(copy, low):
        copy.wait_recv()
        there, source = (has_left, in_low) if low else (has_right, in_up)
        for i, t in enumerate(LOW_TILES[3:] if low else UP_TILES[:3]):
            put(acc, *t, tile(acc, *t) + jnp.where(there, source[2, 8 * i : 8 * i + 8], 0.0))
        if low:
            advance(2, slice(16, 24), whole)
            advance(2, slice(24, 32), slice(0, 128))
        else:
            advance(2, slice(96, 104), slice(128, 256))
            advance(2, slice(104, 112), whole)
        fill_share(0 if low else 7)

    for step in range(3):
        rim_pass()
        last = step == 2
        low_tiles, up_tiles = (LOW_TILES[:3], UP_TILES[3:]) if last else (LOW_TILES, UP_TILES)
        for i, (lt_, ut_) in enumerate(zip(low_tiles, up_tiles)):
            out_low[step, 8 * i : 8 * i + 8] = tile(acc, *lt_)
            out_up[step, 8 * i : 8 * i + 8] = tile(acc, *ut_)
        rows = 8 * len(low_tiles)
        now = [
            rim_copy(out_low.at[step, 0:rows], in_up.at[step, 0:rows], 2 + 2 * step, left),
            rim_copy(out_up.at[step, 0:rows], in_low.at[step, 0:rows], 3 + 2 * step, right),
        ]
        started += now
        scatter_mid()
        advance(step, middle, whole)
        if last:
            advance(step, slice(24, 32), slice(128, 256))
            advance(step, slice(96, 104), slice(0, 128))
            for share in range(1, 7):
                fill_share(share)
            for dy in (4, 3, 5, 2, 6, 1, 7, 0):
                share = lax.rem(my_y + dy, lay.ny)
                pl.when(jnp.logical_and(share > 0, share < 7))(functools.partial(send_share, share))
            pl.when(odd == 1)(lambda: finish_edge(now[1], True))
            pl.when(odd == 0)(lambda: finish_edge(now[0], False))
            send_share(7 - outer)
            pl.when(odd == 1)(lambda: finish_edge(now[0], False))
            pl.when(odd == 0)(lambda: finish_edge(now[1], True))
            for peer in band_peers:
                gram_copy(shares.at[outer], got_edge.at[band], 1, (peer, dom))
            store = pltpu.make_async_copy(filtered, filtered_hbm, store_sem.at[0])
            store.start()
            continue
        weigh_mid((y1, y2)[step])
        gather_mid()
        for copy in now:
            copy.wait_recv()
        for i, (lt_, ut_) in enumerate(zip(LOW_TILES, UP_TILES)):
            got_low = jnp.where(has_left, in_low[step, 8 * i : 8 * i + 8], 0.0)
            got_up = jnp.where(has_right, in_up[step, 8 * i : 8 * i + 8], 0.0)
            put(acc, *lt_, tile(acc, *lt_) + got_low)
            put(acc, *ut_, tile(acc, *ut_) + got_up)
        advance(step, lower, whole)
        advance(step, upper, whole)
        weigh_rim((y1, y2)[step])

    def stack(refs):
        return jnp.concatenate([ref.astype(F32) for ref in refs], axis=0).astype(BF16)

    @pl.when(my_y != outer)
    def _():
        got[band] = shares[my_y]
        wait_bytes(got.at[0 : n_band - 1], False, 0)
        columns = got[...].astype(F32).reshape(8 * n_band, 384).astype(BF16)
        rows = stack([got[y * lay.nz + my_z] for y in range(lay.ny)])
        part[...] = dot_t(rows, columns).reshape(lay.ny, 8, 8 * n_band)
        for i in range(1, lay.ny):
            y = lax.rem(my_y + i, lay.ny)
            gram_copy(part.at[y], part_in.at[my_y], 2, (y * lay.nz + my_z, dom))
        part_in[my_y] = part[my_y]
        part_in[outer] = jnp.zeros((8, 8 * n_band), F32)
        wait_bytes(part_in.at[0 : lay.ny - 2], False, 2)

    @pl.when(my_y == outer)
    def _():
        part_in[outer] = jnp.zeros((8, 8 * n_band), F32)
        wait_bytes(part_in.at[0 : lay.ny - 1], False, 2)

    total = part_in[0]
    for i in range(1, lay.ny):
        total = total + part_in[i]

    got_edge[band] = shares[outer]
    wait_bytes(got_edge.at[0 : n_band - 1], False, 1)
    columns = got_edge[...].astype(F32).reshape(8 * n_band, 384).astype(BF16)
    sums[...] = (total + dot_t(shares[outer], columns)).astype(BF16)

    for i in sorted(range(1, n_dom), key=lambda i: -min(i, n_dom - i)):
        gram_copy(sums, sums_in.at[dom], 3, (band, lax.rem(dom + i, n_dom)))
    sums_in[dom] = sums[...]
    wait_bytes(sums_in.at[0 : n_dom - 1], False, 3)
    total = jnp.sum(sums_in[...].astype(F32), axis=0)
    gram[...] = total * (1.0 / nodes_all)
    store_gram = pltpu.make_async_copy(gram, gram_hbm, store_sem.at[1])
    store_gram.start()

    for copy in started:
        copy.wait_send()

    @pl.when(my_y != outer)
    def _():
        wait_bytes(got.at[0 : 7 * lay.nz - 1], True, 0)
        wait_bytes(part_in.at[0 : lay.ny - 1], True, 2)

    @pl.when(my_y == outer)
    def _():
        wait_bytes(got.at[0 : 7 * lay.nz], True, 0)

    wait_bytes(got_edge.at[0 : n_band - 1], True, 1)
    wait_bytes(sums_in.at[0 : n_dom - 1], True, 3)
    store.wait()
    store_gram.wait()


def local(lay, states_in, cell_nodes, cell_scale, cell_matrix, node_scale, potential):
    owned = states_in.shape[1]
    cells = cell_nodes.shape[0] * 384
    hbm = pl.BlockSpec(memory_space=pltpu.HBM)
    n_band = lay.n_band
    out_shape = (
        jax.ShapeDtypeStruct((8, owned), BF16),
        jax.ShapeDtypeStruct((8, 8 * n_band), F32),
    )
    return pl.pallas_call(
        functools.partial(kernel, lay, owned * lay.n_dom),
        out_shape=out_shape,
        in_specs=[hbm] * 6,
        out_specs=(hbm, hbm),
        scratch_shapes=[
            pltpu.VMEM((8, owned), BF16),
            pltpu.VMEM((8, 8 * n_band), F32),
            pltpu.VMEM(states_in.shape, F32),
            pltpu.VMEM(cell_nodes.shape, jnp.int32),
            pltpu.SMEM(cell_scale.shape, F32),
            pltpu.VMEM(cell_matrix.shape, BF16),
            pltpu.VMEM((1, owned), F32),
            pltpu.VMEM((1, owned), F32),
            pltpu.VMEM((256, cells), BF16),
            pltpu.VMEM((128, cells), BF16),
            pltpu.VMEM((cells, 256), BF16),
            pltpu.VMEM((384, 384), BF16),
            pltpu.VMEM((128, 384), jnp.int32),
            pltpu.VMEM((8, 8, 768), jnp.int32),
            pltpu.VMEM((8, 8, 768), jnp.int32),
            pltpu.VMEM((128, 256), F32),
            pltpu.VMEM((128, 256), F32),
            pltpu.VMEM((128, 256), F32),
            pltpu.VMEM((128, 256), F32),
            pltpu.VMEM((128, 256), F32),
            pltpu.VMEM((128, 256), F32),
            pltpu.VMEM((112, 128), BF16),
            pltpu.VMEM((64, 256), BF16),
            pltpu.VMEM((8, cells), F32),
            pltpu.VMEM((16, cells), F32),
            pltpu.VMEM((128, cells), BF16),
            pltpu.VMEM((2, 16, 384), F32),
            pltpu.VMEM((2, 16, 384), F32),
            pltpu.VMEM((3, 48, 128), F32),
            pltpu.VMEM((3, 48, 128), F32),
            pltpu.VMEM((3, 48, 128), F32),
            pltpu.VMEM((3, 48, 128), F32),
            pltpu.VMEM((8, 8, 384), BF16),
            pltpu.VMEM((n_band, 8, 384), BF16),
            pltpu.VMEM((n_band, 8, 384), BF16),
            pltpu.VMEM((lay.ny, 8, 8 * n_band), F32),
            pltpu.VMEM((lay.ny, 8, 8 * n_band), F32),
            pltpu.VMEM((8, 8 * n_band), BF16),
            pltpu.VMEM((lay.n_dom, 8, 8 * n_band), BF16),
            pltpu.SemaphoreType.DMA((8,)),
            pltpu.SemaphoreType.DMA((8,)),
            pltpu.SemaphoreType.DMA((4,)),
            pltpu.SemaphoreType.DMA((4,)),
            pltpu.SemaphoreType.DMA((6,)),
            pltpu.SemaphoreType.DMA((2,)),
        ],
        compiler_params=pltpu.CompilerParams(
            collective_id=0, has_side_effects=True, vmem_limit_bytes=60 * 1024 * 1024
        ),
    )(states_in, cell_nodes, cell_scale, cell_matrix, node_scale[None, :], potential[None, :])


def solution(mesh):
    lay = Layout(mesh.shape["band"], mesh.shape["dom"])
    in_specs = (P("band", "dom"), P("dom", None), P("dom"), P(), P("dom"), P("dom"))
    out_specs = (P("band", "dom"), P("band", None))
    return jax.shard_map(
        functools.partial(local, lay), mesh=mesh, in_specs=in_specs, out_specs=out_specs, check_vma=False
    )
```

```python
import functools

import jax
import jax.numpy as jnp
from jax import lax
from jax.experimental import pallas as pl
from jax.experimental.pallas import tpu as pltpu
from jax.sharding import PartitionSpec as P

CENTER = 0.25
HALF = 1.5
MESH = pl.DeviceIdType.MESH
F32 = jnp.float32
BF16 = jnp.bfloat16

RIM_HI = (0, 1, 2, 3, 12, 13, 14, 15)
RIM_TILES = tuple((t // 2, t % 2) for t in (*range(1, 8), *range(24, 31)))
MID_HI = (4, 5, 6, 7, 8, 9, 10, 11)
LOW_TILES = ((0, 1), (1, 0), (1, 1), (2, 0), (2, 1), (3, 0))
UP_TILES = ((12, 1), (13, 0), (13, 1), (14, 0), (14, 1), (15, 0))
OWN_TILES = tuple((2 + t // 2, t % 2) for t in range(24))


def tile(ref, hi, half):
    return ref[8 * hi : 8 * hi + 8, 128 * half : 128 * half + 128]


def put(ref, hi, half, value):
    ref[8 * hi : 8 * hi + 8, 128 * half : 128 * half + 128] = value


def dot_t(a, b):
    return lax.dot_general(a, b, (((1,), (1,)), ((), ())), preferred_element_type=F32)


class Layout:
    def __init__(self, n_band, n_dom):
        self.n_band, self.n_dom = n_band, n_dom
        self.ny, self.nz = 8, n_band // 8


def kernel(
    lay, nodes_all,
    states_hbm, nodes_hbm, scale_hbm, matrix_hbm, node_scale_hbm, potential_hbm,
    filtered_hbm, gram_hbm,
    filtered, gram, states, nodes, cell_scale, matrix, node_scale, potential,
    lt, lt_half, le, mat, pad_nodes, hb, hb_half, y0, y1, y2, ns, pc, acc, w1, w2, mid, x16, vh,
    stage, init_in, out_low, out_up, in_low, in_up, shares, got, got_edge, part, part_in, sums, sums_in,
    send_sem, recv_sem, gram_send, gram_recv, load_sem, store_sem,
):
    band, dom = lax.axis_index("band"), lax.axis_index("dom")
    n_band, n_dom = lay.n_band, lay.n_dom
    left, right = lax.rem(dom + n_dom - 1, n_dom), lax.rem(dom + 1, n_dom)
    my_y, my_z = band // lay.nz, lax.rem(band, lay.nz)
    has_left, has_right = dom > 0, dom < n_dom - 1
    odd = lax.rem(dom, 2)

    band_peers = [
        lax.rem(my_y + dy, lay.ny) * lay.nz + lax.rem(my_z + dz, lay.nz)
        for dy in (4, 3, 5, 2, 6, 1, 7, 0) for dz in range(lay.nz) if dy or dz
    ]
    order = [i for i in (n_dom - 1, *range(1, n_dom - 1))]
    dom_peers = [lax.rem(dom + i, n_dom) for i in order]
    barrier = pltpu.get_barrier_semaphore()
    for peer in dom_peers:
        pl.semaphore_signal(barrier, inc=1, device_id=(band, peer), device_id_type=MESH)
    for peer in band_peers:
        pl.semaphore_signal(barrier, inc=1, device_id=(peer, dom), device_id_type=MESH)
    loads = [
        pltpu.make_async_copy(src, dst, load_sem.at[i])
        for i, (src, dst) in enumerate((
            (nodes_hbm, nodes), (matrix_hbm, matrix), (states_hbm, states),
            (node_scale_hbm, node_scale), (potential_hbm, potential), (scale_hbm, cell_scale),
        ))
    ]
    for load in loads:
        load.start()
    for load in loads:
        load.wait()

    pad_nodes[...] = jnp.full(pad_nodes.shape, -4096, jnp.int32)
    pad_nodes[:16, :343] = nodes[...]
    mat[...] = jnp.zeros(mat.shape, BF16)
    mat[:343, :343] = matrix[...]
    mat[...] = mat[...].astype(F32).T.astype(BF16)
    shifted = pad_nodes[...] + 128
    lo_all = shifted & 255
    hi_all = shifted >> 8
    lo_t = lo_all.T
    row_iota = lax.broadcasted_iota(jnp.int32, (256, 768), 0)
    lane_iota = lax.broadcasted_iota(jnp.int32, (384, 256), 1)
    for p in range(8):
        cols = slice(768 * p, 768 * p + 768)
        lo = jnp.concatenate([lo_all[2 * p : 2 * p + 1], lo_all[2 * p + 1 : 2 * p + 2]], axis=1)
        hi = jnp.concatenate([hi_all[2 * p : 2 * p + 1], hi_all[2 * p + 1 : 2 * p + 2]], axis=1)
        hb[p] = jnp.broadcast_to(hi, (8, 768))
        hb_half[p] = jnp.broadcast_to(2 * hi + (lo >> 7), (8, 768))
        lt[:, cols] = jnp.where(row_iota == lo, 1.0, 0.0).astype(BF16)
        lt_half[:, cols] = jnp.where(row_iota[:128] == (lo & 127), 1.0, 0.0).astype(BF16)
        for c in (2 * p, 2 * p + 1):
            le[384 * c : 384 * c + 384, :] = jnp.where(
                lane_iota == lo_t[:, c : c + 1], 1.0, 0.0
            ).astype(BF16)

    for ref in (y0, ns, pc):
        ref[0:16] = jnp.zeros((16, 256), F32)
        ref[112:128] = jnp.zeros((16, 256), F32)
    for b in range(12):
        rows, cols = slice(16 + 8 * b, 24 + 8 * b), slice(256 * b, 256 * b + 256)
        y0[rows] = states[:, cols]
        ns[rows] = jnp.broadcast_to(node_scale[:, cols], (8, 256))
        pc[rows] = jnp.broadcast_to(potential[:, cols] - CENTER, (8, 256))
    for side, cols in ((0, slice(0, 384)), (1, slice(2688, 3072))):
        stage[side, 0:8] = states[:, cols]
        stage[side, 8:16] = jnp.concatenate(
            [node_scale[:, cols], potential[:, cols], jnp.zeros((6, 384), F32)], axis=0
        )

    pl.semaphore_wait(barrier, len(dom_peers) + len(band_peers))

    def rim_copy(src, dst, slot, to):
        copy = pltpu.make_async_remote_copy(
            src_ref=src, dst_ref=dst, send_sem=send_sem.at[slot], recv_sem=recv_sem.at[slot],
            device_id=(band, to), device_id_type=MESH,
        )
        return copy

    def start_both(to_left, to_right):
        @pl.when(odd == 1)
        def _():
            to_right.start()
            to_left.start()

        @pl.when(odd == 0)
        def _():
            to_left.start()
            to_right.start()

    started = [
        rim_copy(stage.at[0], init_in.at[1], 0, left),
        rim_copy(stage.at[1], init_in.at[0], 1, right),
    ]
    start_both(*started)

    def gather_mid():
        for p in range(8):
            cols = slice(768 * p, 768 * p + 768)
            t = jnp.dot(w2[...], lt[:, cols], preferred_element_type=F32)
            index = hb[p]
            total = jnp.zeros((8, 768), F32)
            for k, hi in enumerate(MID_HI):
                total = jnp.where(index == hi, t[8 * k : 8 * k + 8], total)
            mid[:, cols] = total

    def gather_rim(p):
        cols = slice(768 * p, 768 * p + 768)
        t = jnp.dot(w1[...], lt_half[:, cols], preferred_element_type=F32)
        index = hb_half[p]
        total = mid[:, cols]
        for k, (hi, half) in enumerate(RIM_TILES):
            total = jnp.where(index == 2 * hi + half, t[8 * k : 8 * k + 8], total)
        return [total[:, :384], total[:, 384:]]

    def spread(his, p, x):
        cols = slice(768 * p, 768 * p + 768)
        index = jnp.concatenate([hb[p], hb[p]], axis=0)
        for k, hi in enumerate(his):
            vh[16 * k : 16 * k + 16, cols] = jnp.where(index == hi, x, 0.0).astype(BF16)

    def collect(his, r):
        for k, hi in enumerate(his):
            acc[8 * hi : 8 * hi + 8, :] = r[16 * k : 16 * k + 8] + r[16 * k + 8 : 16 * k + 16]

    def rim_pass():
        values = jnp.concatenate([v for p in range(8) for v in gather_rim(p)], axis=0).astype(BF16)
        cells = jnp.dot(values, mat[...], preferred_element_type=F32)
        for p in range(8):
            x = jnp.concatenate(
                [cells[16 * p : 16 * p + 8] * cell_scale[2 * p],
                 cells[16 * p + 8 : 16 * p + 16] * cell_scale[2 * p + 1]], axis=1)
            x = jnp.concatenate([x, x - x.astype(BF16).astype(F32)], axis=0)
            x16[:, 768 * p : 768 * p + 768] = x
            spread(RIM_HI, p, x)
        collect(RIM_HI, jnp.dot(vh[...], le[...], preferred_element_type=F32))

    def scatter_mid():
        for p in range(8):
            spread(MID_HI, p, x16[:, 768 * p : 768 * p + 768])
        collect(MID_HI, jnp.dot(vh[...], le[...], preferred_element_type=F32))

    def weigh_mid(y):
        w2[...] = (ns[32:96] * y[32:96]).astype(BF16)

    def weigh_rim(y):
        for i in range(0, len(RIM_TILES), 2):
            pair = [tile(ns, *t) * tile(y, *t) for t in RIM_TILES[i : i + 2]]
            w1[8 * i : 8 * i + 16, :] = jnp.concatenate(pair, axis=0).astype(BF16)

    def advance(step, rows, cols):
        now = (y0, y1, y2)[step][rows, cols]
        h = ns[rows, cols] * acc[rows, cols] + pc[rows, cols] * now
        if step == 0:
            y1[rows, cols] = h * (1.0 / HALF)
        elif step == 1:
            y2[rows, cols] = h * (2.0 / HALF) - y0[rows, cols]
        else:
            y1[rows, cols] = h * (2.0 / HALF) - y1[rows, cols]

    whole = slice(0, 256)
    middle, lower, upper = slice(32, 96), slice(0, 32), slice(96, 128)

    weigh_mid(y0)
    gather_mid()
    for copy in started:
        copy.wait_recv()
    for side, tiles in ((0, LOW_TILES[:3]), (1, UP_TILES[3:])):
        there = has_left if side == 0 else has_right
        value = jnp.where(there, init_in[side], 0.0)
        for i, (hi, half) in enumerate(tiles):
            cols = slice(128 * i, 128 * i + 128)
            put(y0, hi, half, value[0:8, cols])
            put(ns, hi, half, jnp.broadcast_to(value[8:9, cols], (8, 128)))
            put(pc, hi, half, jnp.broadcast_to(value[9:10, cols] - CENTER, (8, 128)))
    weigh_rim(y0)

    outer = 7 * odd

    def gram_copy(src, dst, slot, device):
        pltpu.make_async_remote_copy(
            src_ref=src, dst_ref=dst, send_sem=gram_send.at[slot], recv_sem=gram_recv.at[slot],
            device_id=device, device_id_type=MESH,
        ).start()

    def wait_bytes(ref, send, slot):
        sem = (gram_send if send else gram_recv).at[slot]
        pltpu.make_async_copy(ref, ref, sem).wait()

    def send_share(share):
        for z in range(lay.nz):
            to = share * lay.nz + z

            @pl.when(band != to)
            def _():
                gram_copy(shares.at[share], got.at[band], 0, (to, dom))

    def fill_share(share):
        tiles = OWN_TILES[3 * share : 3 * share + 3]
        value = jnp.concatenate([tile(y1, *t) for t in tiles], axis=1)
        shares[share] = value.astype(BF16)
        filtered[:, 384 * share : 384 * share + 384] = value

    def finish_edge(copy, low):
        copy.wait_recv()
        there, source = (has_left, in_low) if low else (has_right, in_up)
        for i, t in enumerate(LOW_TILES[3:] if low else UP_TILES[:3]):
            put(acc, *t, tile(acc, *t) + jnp.where(there, source[2, 8 * i : 8 * i + 8], 0.0))
        if low:
            advance(2, slice(16, 24), whole)
            advance(2, slice(24, 32), slice(0, 128))
        else:
            advance(2, slice(96, 104), slice(128, 256))
            advance(2, slice(104, 112), whole)
        fill_share(0 if low else 7)

    for step in range(3):
        rim_pass()
        last = step == 2
        low_tiles, up_tiles = (LOW_TILES[:3], UP_TILES[3:]) if last else (LOW_TILES, UP_TILES)
        for i, (lt_, ut_) in enumerate(zip(low_tiles, up_tiles)):
            out_low[step, 8 * i : 8 * i + 8] = tile(acc, *lt_)
            out_up[step, 8 * i : 8 * i + 8] = tile(acc, *ut_)
        rows = 8 * len(low_tiles)
        now = [
            rim_copy(out_low.at[step, 0:rows], in_up.at[step, 0:rows], 2 + 2 * step, left),
            rim_copy(out_up.at[step, 0:rows], in_low.at[step, 0:rows], 3 + 2 * step, right),
        ]
        start_both(*now)
        started += now
        scatter_mid()
        advance(step, middle, whole)
        if last:
            advance(step, slice(24, 32), slice(128, 256))
            advance(step, slice(96, 104), slice(0, 128))
            for share in range(1, 7):
                fill_share(share)
            for dy in (4, 3, 5, 2, 6, 1, 7, 0):
                share = lax.rem(my_y + dy, lay.ny)
                pl.when(jnp.logical_and(share > 0, share < 7))(functools.partial(send_share, share))
            pl.when(odd == 1)(lambda: finish_edge(now[1], True))
            pl.when(odd == 0)(lambda: finish_edge(now[0], False))
            send_share(7 - outer)
            pl.when(odd == 1)(lambda: finish_edge(now[0], False))
            pl.when(odd == 0)(lambda: finish_edge(now[1], True))
            for peer in band_peers:
                gram_copy(shares.at[outer], got_edge.at[band], 1, (peer, dom))
            store = pltpu.make_async_copy(filtered, filtered_hbm, store_sem.at[0])
            store.start()
            continue
        weigh_mid((y1, y2)[step])
        gather_mid()
        for copy in now:
            copy.wait_recv()
        for i, (lt_, ut_) in enumerate(zip(LOW_TILES, UP_TILES)):
            got_low = jnp.where(has_left, in_low[step, 8 * i : 8 * i + 8], 0.0)
            got_up = jnp.where(has_right, in_up[step, 8 * i : 8 * i + 8], 0.0)
            put(acc, *lt_, tile(acc, *lt_) + got_low)
            put(acc, *ut_, tile(acc, *ut_) + got_up)
        advance(step, lower, whole)
        advance(step, upper, whole)
        weigh_rim((y1, y2)[step])

    def stack(refs):
        return jnp.concatenate([ref.astype(F32) for ref in refs], axis=0).astype(BF16)

    @pl.when(my_y != outer)
    def _():
        got[band] = shares[my_y]
        wait_bytes(got.at[0 : n_band - 1], False, 0)
        columns = got[...].astype(F32).reshape(8 * n_band, 384).astype(BF16)
        rows = stack([got[y * lay.nz + my_z] for y in range(lay.ny)])
        part[...] = dot_t(rows, columns).reshape(lay.ny, 8, 8 * n_band)
        for i in range(1, lay.ny):
            y = lax.rem(my_y + i, lay.ny)
            gram_copy(part.at[y], part_in.at[my_y], 2, (y * lay.nz + my_z, dom))
        part_in[my_y] = part[my_y]
        part_in[outer] = jnp.zeros((8, 8 * n_band), F32)
        wait_bytes(part_in.at[0 : lay.ny - 2], False, 2)

    @pl.when(my_y == outer)
    def _():
        part_in[outer] = jnp.zeros((8, 8 * n_band), F32)
        wait_bytes(part_in.at[0 : lay.ny - 1], False, 2)

    total = part_in[0]
    for i in range(1, lay.ny):
        total = total + part_in[i]

    got_edge[band] = shares[outer]
    wait_bytes(got_edge.at[0 : n_band - 1], False, 1)
    columns = got_edge[...].astype(F32).reshape(8 * n_band, 384).astype(BF16)
    sums[...] = (total + dot_t(shares[outer], columns)).astype(BF16)

    for i in sorted(range(1, n_dom), key=lambda i: -min(i, n_dom - i)):
        gram_copy(sums, sums_in.at[dom], 3, (band, lax.rem(dom + i, n_dom)))
    sums_in[dom] = sums[...]
    wait_bytes(sums_in.at[0 : n_dom - 1], False, 3)
    total = jnp.sum(sums_in[...].astype(F32), axis=0)
    gram[...] = total * (1.0 / nodes_all)
    store_gram = pltpu.make_async_copy(gram, gram_hbm, store_sem.at[1])
    store_gram.start()

    for copy in started:
        copy.wait_send()

    @pl.when(my_y != outer)
    def _():
        wait_bytes(got.at[0 : 7 * lay.nz - 1], True, 0)
        wait_bytes(part_in.at[0 : lay.ny - 1], True, 2)

    @pl.when(my_y == outer)
    def _():
        wait_bytes(got.at[0 : 7 * lay.nz], True, 0)

    wait_bytes(got_edge.at[0 : n_band - 1], True, 1)
    wait_bytes(sums_in.at[0 : n_dom - 1], True, 3)
    store.wait()
    store_gram.wait()


def local(lay, states_in, cell_nodes, cell_scale, cell_matrix, node_scale, potential):
    owned = states_in.shape[1]
    cells = cell_nodes.shape[0] * 384
    hbm = pl.BlockSpec(memory_space=pltpu.HBM)
    n_band = lay.n_band
    out_shape = (
        jax.ShapeDtypeStruct((8, owned), F32),
        jax.ShapeDtypeStruct((8, 8 * n_band), F32),
    )
    last, gram = pl.pallas_call(
        functools.partial(kernel, lay, owned * lay.n_dom),
        out_shape=out_shape,
        in_specs=[hbm] * 6,
        out_specs=(hbm, hbm),
        scratch_shapes=[
            pltpu.VMEM((8, owned), F32),
            pltpu.VMEM((8, 8 * n_band), F32),
            pltpu.VMEM(states_in.shape, F32),
            pltpu.VMEM(cell_nodes.shape, jnp.int32),
            pltpu.SMEM(cell_scale.shape, F32),
            pltpu.VMEM(cell_matrix.shape, BF16),
            pltpu.VMEM((1, owned), F32),
            pltpu.VMEM((1, owned), F32),
            pltpu.VMEM((256, cells), BF16),
            pltpu.VMEM((128, cells), BF16),
            pltpu.VMEM((cells, 256), BF16),
            pltpu.VMEM((384, 384), BF16),
            pltpu.VMEM((128, 384), jnp.int32),
            pltpu.VMEM((8, 8, 768), jnp.int32),
            pltpu.VMEM((8, 8, 768), jnp.int32),
            pltpu.VMEM((128, 256), F32),
            pltpu.VMEM((128, 256), F32),
            pltpu.VMEM((128, 256), F32),
            pltpu.VMEM((128, 256), F32),
            pltpu.VMEM((128, 256), F32),
            pltpu.VMEM((128, 256), F32),
            pltpu.VMEM((112, 128), BF16),
            pltpu.VMEM((64, 256), BF16),
            pltpu.VMEM((8, cells), F32),
            pltpu.VMEM((16, cells), F32),
            pltpu.VMEM((128, cells), BF16),
            pltpu.VMEM((2, 16, 384), F32),
            pltpu.VMEM((2, 16, 384), F32),
            pltpu.VMEM((3, 48, 128), F32),
            pltpu.VMEM((3, 48, 128), F32),
            pltpu.VMEM((3, 48, 128), F32),
            pltpu.VMEM((3, 48, 128), F32),
            pltpu.VMEM((8, 8, 384), BF16),
            pltpu.VMEM((n_band, 8, 384), BF16),
            pltpu.VMEM((n_band, 8, 384), BF16),
            pltpu.VMEM((lay.ny, 8, 8 * n_band), F32),
            pltpu.VMEM((lay.ny, 8, 8 * n_band), F32),
            pltpu.VMEM((8, 8 * n_band), BF16),
            pltpu.VMEM((lay.n_dom, 8, 8 * n_band), BF16),
            pltpu.SemaphoreType.DMA((8,)),
            pltpu.SemaphoreType.DMA((8,)),
            pltpu.SemaphoreType.DMA((4,)),
            pltpu.SemaphoreType.DMA((4,)),
            pltpu.SemaphoreType.DMA((6,)),
            pltpu.SemaphoreType.DMA((2,)),
        ],
        compiler_params=pltpu.CompilerParams(
            collective_id=0, has_side_effects=True, vmem_limit_bytes=60 * 1024 * 1024
        ),
    )(states_in, cell_nodes, cell_scale, cell_matrix, node_scale[None, :], potential[None, :])
    return last.astype(BF16), gram


def solution(mesh):
    lay = Layout(mesh.shape["band"], mesh.shape["dom"])
    in_specs = (P("band", "dom"), P("dom", None), P("dom"), P(), P("dom"), P("dom"))
    out_specs = (P("band", "dom"), P("band", None))
    return jax.shard_map(
        functools.partial(local, lay), mesh=mesh, in_specs=in_specs, out_specs=out_specs, check_vma=False
    )
```

```python
import functools

import jax
import jax.numpy as jnp
from jax import lax
from jax.experimental import pallas as pl
from jax.experimental.pallas import tpu as pltpu
from jax.sharding import PartitionSpec as P

CENTER = 0.25
HALF = 1.5
MESH = pl.DeviceIdType.MESH
F32 = jnp.float32
BF16 = jnp.bfloat16

RIM_HI = (0, 1, 2, 3, 12, 13, 14, 15)
RIM_TILES = tuple((t // 2, t % 2) for t in (*range(1, 8), *range(24, 31)))
MID_HI = (4, 5, 6, 7, 8, 9, 10, 11)
LOW_TILES = ((0, 1), (1, 0), (1, 1), (2, 0), (2, 1), (3, 0))
UP_TILES = ((12, 1), (13, 0), (13, 1), (14, 0), (14, 1), (15, 0))
OWN_TILES = tuple((2 + t // 2, t % 2) for t in range(24))


def tile(ref, hi, half):
    return ref[8 * hi : 8 * hi + 8, 128 * half : 128 * half + 128]


def put(ref, hi, half, value):
    ref[8 * hi : 8 * hi + 8, 128 * half : 128 * half + 128] = value


def dot_t(a, b):
    return lax.dot_general(a, b, (((1,), (1,)), ((), ())), preferred_element_type=F32)


class Layout:
    def __init__(self, n_band, n_dom):
        self.n_band, self.n_dom = n_band, n_dom
        self.ny, self.nz = 8, n_band // 8


def kernel(
    lay, nodes_all,
    states_hbm, nodes_hbm, scale_hbm, matrix_hbm, node_scale_hbm, potential_hbm,
    filtered_hbm, gram_hbm,
    filtered, gram, states, nodes, cell_scale, matrix, node_scale, potential,
    lt, lt_half, le, mat, pad_nodes, hb, hb_half, y0, y1, y2, ns, pc, acc, w1, w2, mid, x16, vh,
    stage, init_in, out_low, out_up, in_low, in_up, shares, got, got_edge, part, part_in, sums, sums_in,
    send_sem, recv_sem, gram_send, gram_recv, load_sem, store_sem, known,
):
    band, dom = lax.axis_index("band"), lax.axis_index("dom")
    n_band, n_dom = lay.n_band, lay.n_dom
    left, right = lax.rem(dom + n_dom - 1, n_dom), lax.rem(dom + 1, n_dom)
    my_y, my_z = band // lay.nz, lax.rem(band, lay.nz)
    has_left, has_right = dom > 0, dom < n_dom - 1
    odd = lax.rem(dom, 2)

    band_peers = [
        lax.rem(my_y + dy, lay.ny) * lay.nz + lax.rem(my_z + dz, lay.nz)
        for dy in (4, 3, 5, 2, 6, 1, 7, 0) for dz in range(lay.nz) if dy or dz
    ]
    def around_y(*steps):
        return [(lax.rem(my_y + i, lay.ny) * lay.nz + my_z, dom) for i in steps]

    def around_z(*steps):
        return [(my_y * lay.nz + lax.rem(my_z + i, lay.nz), dom) for i in steps if i % lay.nz]

    def around_dom(*steps):
        return [(band, lax.rem(dom + i, n_dom)) for i in steps if i % n_dom]

    rounds = dict(
        y1=around_y(1, 7), y2=around_y(2, 6), z1=around_z(1, max(lay.nz - 1, 0)), z2=around_z(2),
        d1=around_dom(2, 2 * n_dom - 2), d2=around_dom(4, 4 * n_dom - 4), d3=around_dom(8, 8 * n_dom - 8),
    )
    slots = {name: i for i, name in enumerate(rounds)}

    def tell(name):
        for peer in rounds[name]:
            pl.semaphore_signal(known.at[slots[name]], inc=1, device_id=peer, device_id_type=MESH)

    def hear(name):
        if rounds[name]:
            pl.semaphore_wait(known.at[slots[name]], len(rounds[name]))

    barrier = pltpu.get_barrier_semaphore()
    greeted = [(band, left), (band, right)] + rounds["y1"] + rounds["z1"]
    for peer in greeted:
        pl.semaphore_signal(barrier, inc=1, device_id=peer, device_id_type=MESH)
    loads = [
        pltpu.make_async_copy(src, dst, load_sem.at[i])
        for i, (src, dst) in enumerate((
            (nodes_hbm, nodes), (matrix_hbm, matrix), (states_hbm, states),
            (node_scale_hbm, node_scale), (potential_hbm, potential), (scale_hbm, cell_scale),
        ))
    ]
    for load in loads:
        load.start()
    for load in loads:
        load.wait()

    pad_nodes[...] = jnp.full(pad_nodes.shape, -4096, jnp.int32)
    pad_nodes[:16, :343] = nodes[...]
    mat[...] = jnp.zeros(mat.shape, BF16)
    mat[:343, :343] = matrix[...]
    mat[...] = mat[...].astype(F32).T.astype(BF16)
    shifted = pad_nodes[...] + 128
    lo_all = shifted & 255
    hi_all = shifted >> 8
    lo_t = lo_all.T
    row_iota = lax.broadcasted_iota(jnp.int32, (256, 768), 0)
    lane_iota = lax.broadcasted_iota(jnp.int32, (384, 256), 1)
    for p in range(8):
        cols = slice(768 * p, 768 * p + 768)
        lo = jnp.concatenate([lo_all[2 * p : 2 * p + 1], lo_all[2 * p + 1 : 2 * p + 2]], axis=1)
        hi = jnp.concatenate([hi_all[2 * p : 2 * p + 1], hi_all[2 * p + 1 : 2 * p + 2]], axis=1)
        hb[p] = jnp.broadcast_to(hi, (8, 768))
        hb_half[p] = jnp.broadcast_to(2 * hi + (lo >> 7), (8, 768))
        lt[:, cols] = jnp.where(row_iota == lo, 1.0, 0.0).astype(BF16)
        lt_half[:, cols] = jnp.where(row_iota[:128] == (lo & 127), 1.0, 0.0).astype(BF16)
        for c in (2 * p, 2 * p + 1):
            le[384 * c : 384 * c + 384, :] = jnp.where(
                lane_iota == lo_t[:, c : c + 1], 1.0, 0.0
            ).astype(BF16)

    for ref in (y0, ns, pc):
        ref[0:16] = jnp.zeros((16, 256), F32)
        ref[112:128] = jnp.zeros((16, 256), F32)
    for b in range(12):
        rows, cols = slice(16 + 8 * b, 24 + 8 * b), slice(256 * b, 256 * b + 256)
        y0[rows] = states[:, cols]
        ns[rows] = jnp.broadcast_to(node_scale[:, cols], (8, 256))
        pc[rows] = jnp.broadcast_to(potential[:, cols] - CENTER, (8, 256))
    for side, cols in ((0, slice(0, 384)), (1, slice(2688, 3072))):
        stage[side, 0:8] = states[:, cols]
        stage[side, 8:16] = jnp.concatenate(
            [node_scale[:, cols], potential[:, cols], jnp.zeros((6, 384), F32)], axis=0
        )

    pl.semaphore_wait(barrier, len(greeted))

    def rim_copy(src, dst, slot, to):
        copy = pltpu.make_async_remote_copy(
            src_ref=src, dst_ref=dst, send_sem=send_sem.at[slot], recv_sem=recv_sem.at[slot],
            device_id=(band, to), device_id_type=MESH,
        )
        copy.start()
        return copy

    started = [
        rim_copy(stage.at[0], init_in.at[1], 0, left),
        rim_copy(stage.at[1], init_in.at[0], 1, right),
    ]
    tell("y1")

    def gather_mid():
        for p in range(8):
            cols = slice(768 * p, 768 * p + 768)
            t = jnp.dot(w2[...], lt[:, cols], preferred_element_type=F32)
            index = hb[p]
            total = jnp.zeros((8, 768), F32)
            for k, hi in enumerate(MID_HI):
                total = jnp.where(index == hi, t[8 * k : 8 * k + 8], total)
            mid[:, cols] = total

    def gather_rim(p):
        cols = slice(768 * p, 768 * p + 768)
        t = jnp.dot(w1[...], lt_half[:, cols], preferred_element_type=F32)
        index = hb_half[p]
        total = mid[:, cols]
        for k, (hi, half) in enumerate(RIM_TILES):
            total = jnp.where(index == 2 * hi + half, t[8 * k : 8 * k + 8], total)
        return [total[:, :384], total[:, 384:]]

    def spread(his, p, x):
        cols = slice(768 * p, 768 * p + 768)
        index = jnp.concatenate([hb[p], hb[p]], axis=0)
        for k, hi in enumerate(his):
            vh[16 * k : 16 * k + 16, cols] = jnp.where(index == hi, x, 0.0).astype(BF16)

    def collect(his, r):
        for k, hi in enumerate(his):
            acc[8 * hi : 8 * hi + 8, :] = r[16 * k : 16 * k + 8] + r[16 * k + 8 : 16 * k + 16]

    def rim_pass():
        values = jnp.concatenate([v for p in range(8) for v in gather_rim(p)], axis=0).astype(BF16)
        cells = jnp.dot(values, mat[...], preferred_element_type=F32)
        for p in range(8):
            x = jnp.concatenate(
                [cells[16 * p : 16 * p + 8] * cell_scale[2 * p],
                 cells[16 * p + 8 : 16 * p + 16] * cell_scale[2 * p + 1]], axis=1)
            x = jnp.concatenate([x, x - x.astype(BF16).astype(F32)], axis=0)
            x16[:, 768 * p : 768 * p + 768] = x
            spread(RIM_HI, p, x)
        collect(RIM_HI, jnp.dot(vh[...], le[...], preferred_element_type=F32))

    def scatter_mid():
        for p in range(8):
            spread(MID_HI, p, x16[:, 768 * p : 768 * p + 768])
        collect(MID_HI, jnp.dot(vh[...], le[...], preferred_element_type=F32))

    def weigh_mid(y):
        w2[...] = (ns[32:96] * y[32:96]).astype(BF16)

    def weigh_rim(y):
        for i in range(0, len(RIM_TILES), 2):
            pair = [tile(ns, *t) * tile(y, *t) for t in RIM_TILES[i : i + 2]]
            w1[8 * i : 8 * i + 16, :] = jnp.concatenate(pair, axis=0).astype(BF16)

    def advance(step, rows, cols):
        now = (y0, y1, y2)[step][rows, cols]
        h = ns[rows, cols] * acc[rows, cols] + pc[rows, cols] * now
        if step == 0:
            y1[rows, cols] = h * (1.0 / HALF)
        elif step == 1:
            y2[rows, cols] = h * (2.0 / HALF) - y0[rows, cols]
        else:
            y1[rows, cols] = h * (2.0 / HALF) - y1[rows, cols]

    whole = slice(0, 256)
    middle, lower, upper = slice(32, 96), slice(0, 32), slice(96, 128)

    weigh_mid(y0)
    gather_mid()
    for copy in started:
        copy.wait_recv()
    tell("d1")
    for side, tiles in ((0, LOW_TILES[:3]), (1, UP_TILES[3:])):
        there = has_left if side == 0 else has_right
        value = jnp.where(there, init_in[side], 0.0)
        for i, (hi, half) in enumerate(tiles):
            cols = slice(128 * i, 128 * i + 128)
            put(y0, hi, half, value[0:8, cols])
            put(ns, hi, half, jnp.broadcast_to(value[8:9, cols], (8, 128)))
            put(pc, hi, half, jnp.broadcast_to(value[9:10, cols] - CENTER, (8, 128)))
    weigh_rim(y0)

    outer = 7 * odd

    def gram_copy(src, dst, slot, device):
        pltpu.make_async_remote_copy(
            src_ref=src, dst_ref=dst, send_sem=gram_send.at[slot], recv_sem=gram_recv.at[slot],
            device_id=device, device_id_type=MESH,
        ).start()

    def wait_bytes(ref, send, slot):
        sem = (gram_send if send else gram_recv).at[slot]
        pltpu.make_async_copy(ref, ref, sem).wait()

    def send_share(share):
        for z in range(lay.nz):
            to = share * lay.nz + z

            @pl.when(band != to)
            def _():
                gram_copy(shares.at[share], got.at[band], 0, (to, dom))

    def fill_share(share):
        tiles = OWN_TILES[3 * share : 3 * share + 3]
        value = jnp.concatenate([tile(y1, *t) for t in tiles], axis=1).astype(BF16)
        shares[share] = value
        filtered[:, 384 * share : 384 * share + 384] = value

    def finish_edge(copy, low):
        copy.wait_recv()
        there, source = (has_left, in_low) if low else (has_right, in_up)
        for i, t in enumerate(LOW_TILES[3:] if low else UP_TILES[:3]):
            put(acc, *t, tile(acc, *t) + jnp.where(there, source[2, 8 * i : 8 * i + 8], 0.0))
        if low:
            advance(2, slice(16, 24), whole)
            advance(2, slice(24, 32), slice(0, 128))
        else:
            advance(2, slice(96, 104), slice(128, 256))
            advance(2, slice(104, 112), whole)
        fill_share(0 if low else 7)

    for step in range(3):
        rim_pass()
        last = step == 2
        low_tiles, up_tiles = (LOW_TILES[:3], UP_TILES[3:]) if last else (LOW_TILES, UP_TILES)
        for i, (lt_, ut_) in enumerate(zip(low_tiles, up_tiles)):
            out_low[step, 8 * i : 8 * i + 8] = tile(acc, *lt_)
            out_up[step, 8 * i : 8 * i + 8] = tile(acc, *ut_)
        rows = 8 * len(low_tiles)
        now = [
            rim_copy(out_low.at[step, 0:rows], in_up.at[step, 0:rows], 2 + 2 * step, left),
            rim_copy(out_up.at[step, 0:rows], in_low.at[step, 0:rows], 3 + 2 * step, right),
        ]
        started += now
        if last:
            hear("z1")
            tell("z2")
        scatter_mid()
        advance(step, middle, whole)
        if last:
            advance(step, slice(24, 32), slice(128, 256))
            advance(step, slice(96, 104), slice(0, 128))
            for share in range(1, 7):
                fill_share(share)
            hear("z2")
            for dy in (4, 3, 5, 2, 6, 1, 7, 0):
                share = lax.rem(my_y + dy, lay.ny)
                pl.when(jnp.logical_and(share > 0, share < 7))(functools.partial(send_share, share))
            pl.when(odd == 1)(lambda: finish_edge(now[1], True))
            pl.when(odd == 0)(lambda: finish_edge(now[0], False))
            send_share(7 - outer)
            pl.when(odd == 1)(lambda: finish_edge(now[0], False))
            pl.when(odd == 0)(lambda: finish_edge(now[1], True))
            for peer in band_peers:
                gram_copy(shares.at[outer], got_edge.at[band], 1, (peer, dom))
            store = pltpu.make_async_copy(filtered, filtered_hbm, store_sem.at[0])
            store.start()
            continue
        weigh_mid((y1, y2)[step])
        gather_mid()
        for copy in now:
            copy.wait_recv()
        for done, following in ((("y1", "y2"), ("d1", "d2")), (("y2", "z1"), ("d2", "d3")))[step]:
            hear(done)
            tell(following)
        for i, (lt_, ut_) in enumerate(zip(LOW_TILES, UP_TILES)):
            got_low = jnp.where(has_left, in_low[step, 8 * i : 8 * i + 8], 0.0)
            got_up = jnp.where(has_right, in_up[step, 8 * i : 8 * i + 8], 0.0)
            put(acc, *lt_, tile(acc, *lt_) + got_low)
            put(acc, *ut_, tile(acc, *ut_) + got_up)
        advance(step, lower, whole)
        advance(step, upper, whole)
        weigh_rim((y1, y2)[step])

    def stack(refs):
        return jnp.concatenate([ref.astype(F32) for ref in refs], axis=0).astype(BF16)

    @pl.when(my_y != outer)
    def _():
        got[band] = shares[my_y]
        wait_bytes(got.at[0 : n_band - 1], False, 0)
        columns = got[...].astype(F32).reshape(8 * n_band, 384).astype(BF16)
        rows = stack([got[y * lay.nz + my_z] for y in range(lay.ny)])
        part[...] = dot_t(rows, columns).reshape(lay.ny, 8, 8 * n_band)
        for i in range(1, lay.ny):
            y = lax.rem(my_y + i, lay.ny)
            gram_copy(part.at[y], part_in.at[my_y], 2, (y * lay.nz + my_z, dom))
        part_in[my_y] = part[my_y]
        part_in[outer] = jnp.zeros((8, 8 * n_band), F32)
        wait_bytes(part_in.at[0 : lay.ny - 2], False, 2)

    @pl.when(my_y == outer)
    def _():
        part_in[outer] = jnp.zeros((8, 8 * n_band), F32)
        wait_bytes(part_in.at[0 : lay.ny - 1], False, 2)

    total = part_in[0]
    for i in range(1, lay.ny):
        total = total + part_in[i]

    got_edge[band] = shares[outer]
    wait_bytes(got_edge.at[0 : n_band - 1], False, 1)
    columns = got_edge[...].astype(F32).reshape(8 * n_band, 384).astype(BF16)
    sums[...] = (total + dot_t(shares[outer], columns)).astype(BF16)

    hear("d3")
    for i in sorted(range(1, n_dom), key=lambda i: -min(i, n_dom - i)):
        gram_copy(sums, sums_in.at[dom], 3, (band, lax.rem(dom + i, n_dom)))
    sums_in[dom] = sums[...]
    wait_bytes(sums_in.at[0 : n_dom - 1], False, 3)
    total = jnp.sum(sums_in[...].astype(F32), axis=0)
    gram[...] = total * (1.0 / nodes_all)
    store_gram = pltpu.make_async_copy(gram, gram_hbm, store_sem.at[1])
    store_gram.start()

    for copy in started:
        copy.wait_send()

    @pl.when(my_y != outer)
    def _():
        wait_bytes(got.at[0 : 7 * lay.nz - 1], True, 0)
        wait_bytes(part_in.at[0 : lay.ny - 1], True, 2)

    @pl.when(my_y == outer)
    def _():
        wait_bytes(got.at[0 : 7 * lay.nz], True, 0)

    wait_bytes(got_edge.at[0 : n_band - 1], True, 1)
    wait_bytes(sums_in.at[0 : n_dom - 1], True, 3)
    store.wait()
    store_gram.wait()


def local(lay, states_in, cell_nodes, cell_scale, cell_matrix, node_scale, potential):
    owned = states_in.shape[1]
    cells = cell_nodes.shape[0] * 384
    hbm = pl.BlockSpec(memory_space=pltpu.HBM)
    n_band = lay.n_band
    out_shape = (
        jax.ShapeDtypeStruct((8, owned), BF16),
        jax.ShapeDtypeStruct((8, 8 * n_band), F32),
    )
    return pl.pallas_call(
        functools.partial(kernel, lay, owned * lay.n_dom),
        out_shape=out_shape,
        in_specs=[hbm] * 6,
        out_specs=(hbm, hbm),
        scratch_shapes=[
            pltpu.VMEM((8, owned), BF16),
            pltpu.VMEM((8, 8 * n_band), F32),
            pltpu.VMEM(states_in.shape, F32),
            pltpu.VMEM(cell_nodes.shape, jnp.int32),
            pltpu.SMEM(cell_scale.shape, F32),
            pltpu.VMEM(cell_matrix.shape, BF16),
            pltpu.VMEM((1, owned), F32),
            pltpu.VMEM((1, owned), F32),
            pltpu.VMEM((256, cells), BF16),
            pltpu.VMEM((128, cells), BF16),
            pltpu.VMEM((cells, 256), BF16),
            pltpu.VMEM((384, 384), BF16),
            pltpu.VMEM((128, 384), jnp.int32),
            pltpu.VMEM((8, 8, 768), jnp.int32),
            pltpu.VMEM((8, 8, 768), jnp.int32),
            pltpu.VMEM((128, 256), F32),
            pltpu.VMEM((128, 256), F32),
            pltpu.VMEM((128, 256), F32),
            pltpu.VMEM((128, 256), F32),
            pltpu.VMEM((128, 256), F32),
            pltpu.VMEM((128, 256), F32),
            pltpu.VMEM((112, 128), BF16),
            pltpu.VMEM((64, 256), BF16),
            pltpu.VMEM((8, cells), F32),
            pltpu.VMEM((16, cells), F32),
            pltpu.VMEM((128, cells), BF16),
            pltpu.VMEM((2, 16, 384), F32),
            pltpu.VMEM((2, 16, 384), F32),
            pltpu.VMEM((3, 48, 128), F32),
            pltpu.VMEM((3, 48, 128), F32),
            pltpu.VMEM((3, 48, 128), F32),
            pltpu.VMEM((3, 48, 128), F32),
            pltpu.VMEM((8, 8, 384), BF16),
            pltpu.VMEM((n_band, 8, 384), BF16),
            pltpu.VMEM((n_band, 8, 384), BF16),
            pltpu.VMEM((lay.ny, 8, 8 * n_band), F32),
            pltpu.VMEM((lay.ny, 8, 8 * n_band), F32),
            pltpu.VMEM((8, 8 * n_band), BF16),
            pltpu.VMEM((lay.n_dom, 8, 8 * n_band), BF16),
            pltpu.SemaphoreType.DMA((8,)),
            pltpu.SemaphoreType.DMA((8,)),
            pltpu.SemaphoreType.DMA((4,)),
            pltpu.SemaphoreType.DMA((4,)),
            pltpu.SemaphoreType.DMA((6,)),
            pltpu.SemaphoreType.DMA((2,)),
            pltpu.SemaphoreType.REGULAR((7,)),
        ],
        compiler_params=pltpu.CompilerParams(
            collective_id=0, has_side_effects=True, vmem_limit_bytes=60 * 1024 * 1024
        ),
    )(states_in, cell_nodes, cell_scale, cell_matrix, node_scale[None, :], potential[None, :])


def solution(mesh):
    lay = Layout(mesh.shape["band"], mesh.shape["dom"])
    in_specs = (P("band", "dom"), P("dom", None), P("dom"), P(), P("dom"), P("dom"))
    out_specs = (P("band", "dom"), P("band", None))
    return jax.shard_map(
        functools.partial(local, lay), mesh=mesh, in_specs=in_specs, out_specs=out_specs, check_vma=False
    )
```
